128 devices in a mesh: dp: 8 (over z, x_lo), frame: 16 (over y, x_hi, core).
Axes of the slice: x: 4 (x_hi: 2, x_lo: 2; x = x_hi * 2 + x_lo), y: 4, z: 4, core: 2. Of those that a mesh axis runs over, the one named last changes fastest.
Arguments:
- latents: bfloat16 [128, 1024, 256], P(('dp', 'frame')), parts along dimension 0, may hold values from -6 to 6
- cotangent: bfloat16 [128, 1024, 256], P(('dp', 'frame')), parts along dimension 0, may hold values from -6 to 6
- gain_time: float32 [256], replicated, may hold values from 0.5 to 1.5
- qkv_time: bfloat16 [256, 768], replicated, may hold values from -3 to 3, as said below
- out_time: bfloat16 [256, 256], replicated, may hold values from -0.375 to 0.375
- gain_space: float32 [256], replicated, may hold values from 0.5 to 1.5
- qkv_space: bfloat16 [256, 768], replicated, may hold values from -3 to 3, as said below
- out_space: bfloat16 [256, 256], replicated, may hold values from -0.375 to 0.375
Outputs:
- grad_latents: float32 [128, 1024, 256], P(('dp', 'frame')), parts along dimension 0
- grad_qkv_time: float32 [2048, 768], P(('dp', 'frame')), parts along dimension 0
- grad_out_time: float32 [2048, 256], P(('dp', 'frame')), parts along dimension 0
- grad_qkv_space: float32 [2048, 768], P(('dp', 'frame')), parts along dimension 0
- grad_out_space: float32 [2048, 256], P(('dp', 'frame')), parts along dimension 0
- grad_gain_time: float32 [2048], P(('dp', 'frame')), parts along dimension 0
- grad_gain_space: float32 [2048], P(('dp', 'frame')), parts along dimension 0
The draws below stay inside these ranges and needn't reach their ends.
There are 8 independent parts, one for each index of `dp`. The reference program is written for one: setup_inputs(seed, part) draws one part's arguments, and reference() takes and returns one part's arrays. A program takes and returns all parts, laid end to end along the dimension named above; an argument that names none is the same for every part. Nothing has to cross between parts.
Inputs may be any that keep to these rules, and one draw needn't show every extreme that they name: `qkv_time`: entries of a projection scaled by fan-in. `qkv_space`: entries of a projection scaled by fan-in.
All inputs are finite; a program needn't handle non-finite values.
Results may differ from the reference program's by a relative error of at most 0.035.
Values may be sent and summed in bfloat16 or wider, within the bound.
No kernel may reach another device: no remote copies, remote signals or barrier semaphores. Data moves between devices by JAX's collectives and lax.ppermute only.
A program may use at most 128 MiB of HBM per device.

```python
import jax
import jax.numpy as jnp
from jax import lax

HEADS = 8
HEAD_DIM = 32
D = 256
WIN = 8
HH = 32
WW = 32
FRAMES = 16
TOKENS_FRAME = 1024


def boosted_projection(key, boost):
    weights = jax.random.truncated_normal(key, -4.0, 4.0, (D, 3 * D), jnp.float32) * D ** (-0.5)
    columns = jnp.arange(3 * D)
    factor = jnp.where(columns < 2 * D, boost, 1.0)
    return (weights * factor[None, :]).astype(jnp.bfloat16)


def draw_qkv_time(key, part):
    key = jax.random.fold_in(key, 11)
    return boosted_projection(key, 1.0)


def draw_qkv_space(key, part):
    key = jax.random.fold_in(key, 23)
    return boosted_projection(key, 1.0)


def block_levels(rng, extent, cuts, least, top_value):
    level = 1.0
    for dim, parts in cuts:
        draws = jax.random.uniform(jax.random.fold_in(jax.random.fold_in(rng, 6), dim), (parts,), jnp.float32, least / len(cuts), top_value / len(cuts))
        level = level * jnp.repeat(jnp.exp(draws), extent[dim] // parts).reshape((-1,) + (1,) * (len(extent) - 1 - dim))
    return level


def normal_values(own_key, dims, spread, limit, pieces=(), held_as=jnp.bfloat16):
    level = block_levels(own_key, dims, pieces, -0.22, 0.18) if pieces else 1.0
    result = jax.random.normal(own_key, dims, jnp.float32) * spread * level
    return jnp.minimum(jnp.maximum(result, -limit), limit).astype(held_as)


def setup_inputs(seed: int = 0, part: int = 0) -> dict:
    key_list = jax.random.split(jax.random.key(seed), 9)
    own_keys = jax.random.split(jax.random.fold_in(key_list[8], part), 9)
    latents = normal_values(own_keys[0], (FRAMES, TOKENS_FRAME, D), 1.0, 6.0, ((0, 16),))
    cotangent = normal_values(own_keys[1], (FRAMES, TOKENS_FRAME, D), 1.0, 6.0, ((0, 16),))
    gain_time = jnp.clip(1.0 + 0.1 * jax.random.normal(key_list[2], (D,), jnp.float32), 0.5, 1.5)
    qkv_time = draw_qkv_time(jax.random.fold_in(key_list[8], 71), part)
    out_time = normal_values(key_list[4], (D, D), D ** -0.5, 0.375)
    gain_space = jnp.clip(1.0 + 0.1 * jax.random.normal(key_list[5], (D,), jnp.float32), 0.5, 1.5)
    qkv_space = draw_qkv_space(jax.random.fold_in(key_list[8], 71), part)
    out_space = normal_values(key_list[7], (D, D), D ** -0.5, 0.375)
    return dict(latents=latents, cotangent=cotangent, gain_time=gain_time, qkv_time=qkv_time, out_time=out_time, gain_space=gain_space, qkv_space=qkv_space, out_space=out_space)


EPSILON = 1e-06

def norm_stats(values_in):
    floats = values_in.astype(jnp.float32)
    factor = lax.rsqrt(lax.optimization_barrier(jnp.mean(floats * floats, -1, keepdims=True)) + EPSILON)
    return (floats * factor, factor)

def norm_back(grad_in, normed, factor, gain):
    scaled = grad_in * gain
    grad_out = factor * (scaled - normed * lax.optimization_barrier(jnp.mean(scaled * normed, -1, keepdims=True)))
    return (grad_out, lax.optimization_barrier(jnp.sum(grad_in * normed, axis=0)))

def temporal_attention(queries, keys_in, values_in):
    score_scale = queries.shape[-1] ** (-0.5)
    scores = jnp.einsum('fshd,gshd->shfg', queries.astype(jnp.float32), keys_in.astype(jnp.float32)) * score_scale
    probs = jax.nn.softmax(scores, -1).astype(jnp.bfloat16)
    return jnp.einsum('shfg,gshd->fshd', probs.astype(jnp.float32), values_in.astype(jnp.float32)).astype(jnp.bfloat16)

def window_attention(queries, keys_in, values_in):
    score_scale = queries.shape[-1] ** (-0.5)
    scores = jnp.einsum('bihd,bjhd->bhij', queries.astype(jnp.float32), keys_in.astype(jnp.float32)) * score_scale
    probs = jax.nn.softmax(scores, -1).astype(jnp.bfloat16)
    return jnp.einsum('bhij,bjhd->bihd', probs.astype(jnp.float32), values_in.astype(jnp.float32)).astype(jnp.bfloat16)

def to_windows(tensor, frames):
    chans = tensor.shape[-1]
    shaped = tensor.reshape(frames, HH // WIN, WIN, WW // WIN, WIN, chans)
    return shaped.transpose(0, 1, 3, 2, 4, 5).reshape(-1, WIN * WIN, chans)

def from_windows(tensor, frames):
    chans = tensor.shape[-1]
    shaped = tensor.reshape(frames, HH // WIN, WW // WIN, WIN, WIN, chans)
    return shaped.transpose(0, 1, 3, 2, 4, 5).reshape(frames * HH * WW, chans)

def reference(latents, cotangent, gain_time, qkv_time, out_time, gain_space, qkv_space, out_space):
    frames, tokens, model_width = latents.shape
    row_count = frames * tokens
    flat_in = latents.reshape(row_count, model_width)
    normed_time, factor_time = norm_stats(flat_in)
    input_time = (normed_time * gain_time).astype(jnp.bfloat16)
    proj_time = jnp.dot(input_time, qkv_time, preferred_element_type=jnp.float32).astype(jnp.bfloat16)
    split_time = proj_time.reshape(frames, tokens, 3, HEADS, HEAD_DIM)
    mixed_t, back_time = jax.vjp(temporal_attention, split_time[:, :, 0], split_time[:, :, 1], split_time[:, :, 2])
    mixed_time = mixed_t.reshape(row_count, model_width)
    middle = (flat_in.astype(jnp.float32) + jnp.dot(mixed_time, out_time, preferred_element_type=jnp.float32)).astype(jnp.bfloat16)
    normed_space, factor_space = norm_stats(middle)
    input_space = (normed_space * gain_space).astype(jnp.bfloat16)
    proj_space = jnp.dot(input_space, qkv_space, preferred_element_type=jnp.float32).astype(jnp.bfloat16)
    windowed = to_windows(proj_space.reshape(frames, tokens, 3 * model_width), frames)
    windowed = windowed.reshape(windowed.shape[0], WIN * WIN, 3, HEADS, HEAD_DIM)
    mixed_w, back_space = jax.vjp(window_attention, windowed[:, :, 0], windowed[:, :, 1], windowed[:, :, 2])
    mixed_space = from_windows(mixed_w.reshape(-1, WIN * WIN, model_width), frames)
    flat_cot = cotangent.reshape(row_count, model_width)
    sum_out_space = jnp.dot(mixed_space.T, flat_cot, preferred_element_type=jnp.float32)
    dmixed_space = jnp.dot(flat_cot, out_space.T, preferred_element_type=jnp.float32).astype(jnp.bfloat16)
    dmix_win = to_windows(dmixed_space.reshape(frames, tokens, model_width), frames)
    grads_w = back_space(dmix_win.reshape(-1, WIN * WIN, HEADS, HEAD_DIM))
    stacked_w = jnp.stack(grads_w, 2).reshape(-1, WIN * WIN, 3 * model_width)
    dproj_space = from_windows(stacked_w, frames)
    sum_qkv_space = jnp.dot(input_space.T, dproj_space, preferred_element_type=jnp.float32)
    dinput_space = jnp.dot(dproj_space, qkv_space.T, preferred_element_type=jnp.float32)
    dnorm_space, sum_gain_space = norm_back(dinput_space, normed_space, factor_space, gain_space)
    dmiddle = flat_cot.astype(jnp.float32) + dnorm_space
    dmiddle_round = dmiddle.astype(jnp.bfloat16)
    sum_out_time = jnp.dot(mixed_time.T, dmiddle_round, preferred_element_type=jnp.float32)
    dmixed_time = jnp.dot(dmiddle_round, out_time.T, preferred_element_type=jnp.float32).astype(jnp.bfloat16)
    grads_t = back_time(dmixed_time.reshape(frames, tokens, HEADS, HEAD_DIM))
    dproj_time = jnp.stack(grads_t, 2).reshape(row_count, 3 * model_width)
    sum_qkv_time = jnp.dot(input_time.T, dproj_time, preferred_element_type=jnp.float32)
    dinput_time = jnp.dot(dproj_time, qkv_time.T, preferred_element_type=jnp.float32)
    dnorm_time, sum_gain_time = norm_back(dinput_time, normed_time, factor_time, gain_time)
    grad_latents = (dmiddle + dnorm_time).reshape(frames, tokens, model_width)
    inverse = 1.0 / jnp.sqrt(jnp.float32(frames * tokens))
    return (grad_latents, sum_qkv_time * inverse, sum_out_time * inverse, sum_qkv_space * inverse, sum_out_space * inverse, sum_gain_time * inverse, sum_gain_space * inverse)
```

```python
import functools

import jax
import jax.numpy as jnp
from jax import lax
from jax.experimental import pallas as pl
from jax.experimental.pallas import tpu as pltpu
from jax.sharding import PartitionSpec as P

HEADS = 8
HEAD_DIM = 32
D = 256
WIN = 8
HH = 32
WW = 32
FRAMES = 16
TOKENS = 1024
ROWS = 1024
SHARE = 64
GROUP = 128
HALF = 128
PACK = 4
CHUNK = 256
EPSILON = 1e-06
SCALE = HEAD_DIM ** (-0.5)
MASKED = -1e30
F32 = jnp.float32
BF16 = jnp.bfloat16


def dot_nn(a, b):
    return lax.dot_general(a, b, (((1,), (0,)), ((), ())), preferred_element_type=F32)


def dot_nt(a, b):
    return lax.dot_general(a, b, (((1,), (1,)), ((), ())), preferred_element_type=F32)


def dot_tn(a, b):
    return lax.dot_general(a, b, (((0,), (0,)), ((), ())), preferred_element_type=F32)


def head_masks():
    lane = lax.broadcasted_iota(jnp.int32, (1, HALF), 1) // HEAD_DIM
    return [(lane == h).astype(F32).astype(BF16) for h in range(PACK)]


def spread(x, masks):
    return jnp.concatenate([x * m for m in masks], axis=0)


def flip(x):
    return jnp.concatenate([x[:, GROUP * h : GROUP * (h + 1)].T for h in range(PACK)], axis=1)


def soft_probs(q, k, masks, bias):
    qb = spread(q, masks)
    scores = dot_nt(k, qb) * SCALE + bias
    top = jnp.max(scores, axis=0, keepdims=True)
    ex = jnp.exp(scores - top)
    return ex * (1.0 / jnp.sum(ex, axis=0, keepdims=True)), qb


def mix(probs, v, masks):
    return dot_nn(flip(probs), spread(v, masks)).astype(BF16)


def attend_back(q, k, v, do, probs, qb, masks):
    dob = spread(do, masks)
    dv = dot_nn(probs.astype(BF16), dob)
    dp = dot_nt(v, dob)
    weighted = probs.astype(F32) * dp
    inner = jnp.sum(weighted, axis=0, keepdims=True)
    ds = (weighted - probs.astype(F32) * inner).astype(BF16)
    dk = dot_nn(ds, qb) * SCALE
    dq = dot_nn(flip(ds), spread(k, masks)) * SCALE
    return dq.astype(BF16), dk.astype(BF16), dv.astype(BF16)


def norm_factor(x):
    return lax.rsqrt(jnp.mean(x * x, -1, keepdims=True) + EPSILON)


def main_kernel(
    moved, gain_t, qkv_t, out_t, gain_s, qkv_s, out_s, sent,
    xs, cots, proj_t, probs_t, mixed_t, middle, proj_s, mixed_s, dmix, dproj, dmid, grads, in_t, in_s,
):
    masks = head_masks()
    row = lax.broadcasted_iota(jnp.int32, (GROUP, PACK * GROUP), 0)
    col = lax.broadcasted_iota(jnp.int32, (GROUP, PACK * GROUP), 1)
    bias_t = jnp.where(row % WIN == col % WIN, 0.0, MASKED).astype(F32)
    bias_s = jnp.where((row // WIN) % 2 == (col // WIN) % 2, 0.0, MASKED).astype(F32)

    def reorder(f, _):
        for p in range(SHARE // 16):
            for src, dst, base in ((moved, xs, 0), (moved, cots, SHARE)):
                both = src[f, base + 16 * p : base + 16 * (p + 1), :].astype(F32)
                dst[pl.ds(pl.multiple_of(2 * p * GROUP + f * WIN, WIN), WIN), :] = both[:WIN]
                dst[pl.ds(pl.multiple_of((2 * p + 1) * GROUP + f * WIN, WIN), WIN), :] = both[WIN:]
        return _

    lax.fori_loop(0, FRAMES, reorder, 0)

    def rows_of(c):
        return pl.ds(pl.multiple_of(c * CHUNK, CHUNK), CHUNK)

    def pair_of(c):
        return pl.ds(2 * c, 2)

    def fold(x):
        return x.reshape(2, GROUP, x.shape[1])

    def project_time(c, _):
        x = xs[rows_of(c), :]
        inp = (x * norm_factor(x) * gain_t[...]).astype(BF16)
        in_t[rows_of(c), :] = inp
        proj_t[rows_of(c), :] = dot_nn(inp, qkv_t[...]).astype(BF16)
        return _

    lax.fori_loop(0, ROWS // CHUNK, project_time, 0)

    def time_forward(t, _):
        rows = pl.ds(pl.multiple_of(t * GROUP, GROUP), GROUP)
        for half in range(2):
            lanes = slice(HALF * half, HALF * (half + 1))
            q = proj_t[rows, lanes]
            k = proj_t[rows, D + HALF * half : D + HALF * (half + 1)]
            v = proj_t[rows, 2 * D + HALF * half : 2 * D + HALF * (half + 1)]
            probs, qb = soft_probs(q, k, masks, bias_t)
            probs = probs.astype(BF16)
            probs_t[2 * t + half] = probs
            mixed_t[rows, lanes] = mix(probs, v, masks)
        return _

    lax.fori_loop(0, ROWS // GROUP, time_forward, 0)

    def project_space(c, _):
        mid = (xs[rows_of(c), :] + dot_nn(mixed_t[rows_of(c), :], out_t[...])).astype(BF16)
        middle[rows_of(c), :] = mid
        mid = mid.astype(F32)
        inp = (mid * norm_factor(mid) * gain_s[...]).astype(BF16)
        in_s[rows_of(c), :] = inp
        proj_s[pair_of(c)] = fold(dot_nn(inp, qkv_s[...]).astype(BF16))
        dmix[pair_of(c)] = fold(dot_nt(cots[rows_of(c), :].astype(BF16), out_s[...]).astype(BF16))
        return _

    lax.fori_loop(0, ROWS // CHUNK, project_space, 0)

    def space(g, _):
        rows = pl.ds(pl.multiple_of(g * 16, 16), 16)

        def take(ref, first):
            return ref[:, rows, first : first + HALF].reshape(GROUP, HALF)

        def put(ref, first, x):
            ref[:, rows, first : first + HALF] = x.reshape(ROWS // GROUP, 16, HALF)

        for half in range(2):
            first = HALF * half
            q, k, v = (take(proj_s, D * i + first) for i in range(3))
            probs, qb = soft_probs(q, k, masks, bias_s)
            put(mixed_s, first, mix(probs.astype(BF16), v, masks))
            grad3 = attend_back(q, k, v, take(dmix, first), probs, qb, masks)
            for i in range(3):
                put(dproj, D * i + first, grad3[i])
        return _

    lax.fori_loop(0, FRAMES // 2, space, 0)

    def place(first, sums):
        sums = sums.astype(BF16)
        for d in range(FRAMES):
            sent[d, first : first + 16, :] = sums[16 * d : 16 * (d + 1), :]

    for i in range(3):
        place(128 + 16 * i, dot_tn(in_s[...], dproj[:, :, D * i : D * (i + 1)].reshape(ROWS, D)))
    place(128 + 48, dot_tn(mixed_s[...].reshape(ROWS, D), cots[...].astype(BF16)))

    def middle_back(c, gain_sum):
        dinput = dot_nt(dproj[pair_of(c)].reshape(CHUNK, 3 * D), qkv_s[...])
        mid = middle[rows_of(c), :].astype(F32)
        factor = norm_factor(mid)
        normed = mid * factor
        scaled = dinput * gain_s[...]
        dm = cots[rows_of(c), :] + factor * (
            scaled - normed * jnp.mean(scaled * normed, -1, keepdims=True)
        )
        dmid[rows_of(c), :] = dm
        dmix[pair_of(c)] = fold(dot_nt(dm.astype(BF16), out_t[...]).astype(BF16))
        return gain_sum + jnp.sum(dinput * normed, axis=0, keepdims=True)

    gain_sum_s = lax.fori_loop(0, ROWS // CHUNK, middle_back, jnp.zeros((1, D), F32))

    def time_back(t, _):
        rows = pl.ds(pl.multiple_of(t * GROUP, GROUP), GROUP)
        for half in range(2):
            first = HALF * half
            q, k, v = (proj_t[rows, D * i + first : D * i + first + HALF] for i in range(3))
            grad3 = attend_back(
                q, k, v, dmix[t, :, first : first + HALF], probs_t[2 * t + half], spread(q, masks), masks
            )
            for i in range(3):
                dproj[t, :, D * i + first : D * i + first + HALF] = grad3[i]
        return _

    lax.fori_loop(0, ROWS // GROUP, time_back, 0)

    for i in range(3):
        place(64 + 16 * i, dot_tn(in_t[...], dproj[:, :, D * i : D * (i + 1)].reshape(ROWS, D)))
    place(64 + 48, dot_tn(mixed_t[...], dmid[...].astype(BF16)))

    def input_back(c, gain_sum):
        dinput = dot_nt(dproj[pair_of(c)].reshape(CHUNK, 3 * D), qkv_t[...])
        x = xs[rows_of(c), :]
        factor = norm_factor(x)
        normed = x * factor
        scaled = dinput * gain_t[...]
        grads[rows_of(c), :] = dmid[rows_of(c), :] + factor * (
            scaled - normed * jnp.mean(scaled * normed, -1, keepdims=True)
        )
        return gain_sum + jnp.sum(dinput * normed, axis=0, keepdims=True)

    gain_sum_t = lax.fori_loop(0, ROWS // CHUNK, input_back, jnp.zeros((1, D), F32))

    gains = jnp.concatenate([gain_sum_t, gain_sum_s], axis=0)
    high = gains.astype(BF16).astype(F32)
    low = gains - high
    extra = jnp.concatenate([high, low, jnp.zeros((12, D), F32)], axis=0).astype(BF16)

    def restore(f, _):
        for p in range(SHARE // 16):
            first = grads[pl.ds(pl.multiple_of(2 * p * GROUP + f * WIN, WIN), WIN), :]
            second = grads[pl.ds(pl.multiple_of((2 * p + 1) * GROUP + f * WIN, WIN), WIN), :]
            sent[f, 16 * p : 16 * (p + 1), :] = jnp.concatenate([first, second], axis=0).astype(BF16)
        sent[f, 192:208, :] = extra
        return _

    lax.fori_loop(0, FRAMES, restore, 0)


def run_main(moved, gain_t, qkv_t, out_t, gain_s, qkv_s, out_s):
    return pl.pallas_call(
        main_kernel,
        out_shape=jax.ShapeDtypeStruct((FRAMES, 208, D), BF16),
        scratch_shapes=[
            pltpu.VMEM((ROWS, D), F32),
            pltpu.VMEM((ROWS, D), F32),
            pltpu.VMEM((ROWS, 3 * D), BF16),
            pltpu.VMEM((16, GROUP, PACK * GROUP), BF16),
            pltpu.VMEM((ROWS, D), BF16),
            pltpu.VMEM((ROWS, D), BF16),
            pltpu.VMEM((ROWS // GROUP, GROUP, 3 * D), BF16),
            pltpu.VMEM((ROWS // GROUP, GROUP, D), BF16),
            pltpu.VMEM((ROWS // GROUP, GROUP, D), BF16),
            pltpu.VMEM((ROWS // GROUP, GROUP, 3 * D), BF16),
            pltpu.VMEM((ROWS, D), F32),
            pltpu.VMEM((ROWS, D), F32),
            pltpu.VMEM((ROWS, D), BF16),
            pltpu.VMEM((ROWS, D), BF16),
        ],
        compiler_params=pltpu.CompilerParams(vmem_limit_bytes=40 * 1024 * 1024),
        cost_estimate=pl.CostEstimate(
            flops=8 * 10**9, bytes_accessed=6 * 10**6, transcendentals=2 * 10**6
        ),
    )(moved, gain_t.reshape(1, D), qkv_t, out_t, gain_s.reshape(1, D), qkv_s, out_s)


def to_windows(frame):
    split = frame.reshape(HH // WIN, WIN, WW // WIN, WIN, D)
    return split.transpose(0, 2, 1, 3, 4).reshape(FRAMES, SHARE, D)


def from_windows(windows):
    split = windows.reshape(HH // WIN, WW // WIN, WIN, WIN, D)
    return split.transpose(0, 2, 1, 3, 4).reshape(1, TOKENS, D)


def exchange(x):
    return lax.all_to_all(x, "frame", split_axis=0, concat_axis=0, tiled=True)


def per_device(latents, cotangent, gain_time, qkv_time, out_time, gain_space, qkv_space, out_space):
    moved = exchange(jnp.concatenate([to_windows(latents), to_windows(cotangent)], axis=1))
    sent = run_main(moved, gain_time, qkv_time, out_time, gain_space, qkv_space, out_space)
    back = exchange(sent).astype(F32)
    grad_latents = from_windows(back[:, :SHARE])
    inverse = 1.0 / jnp.sqrt(jnp.float32(FRAMES * TOKENS))
    sums = jnp.sum(back[:, SHARE:], axis=0) * inverse

    def weights(first):
        qkv = jnp.concatenate([sums[first + 16 * i : first + 16 * (i + 1)] for i in range(3)], axis=1)
        return qkv, sums[first + 48 : first + 64]

    qkv_t, out_t = weights(0)
    qkv_s, out_s = weights(64)
    mine = lax.axis_index("frame") * 16
    gains = lax.dynamic_slice_in_dim(sums[128:130] + sums[130:132], mine, 16, axis=1)
    return (grad_latents, qkv_t, out_t, qkv_s, out_s, gains[0], gains[1])


def solution(mesh):
    whole = P(("dp", "frame"), None, None)
    rows = P(("dp", "frame"), None)
    flat = P(("dp", "frame"))
    return jax.shard_map(
        per_device,
        mesh=mesh,
        in_specs=(whole, whole, P(), P(), P(), P(), P(), P()),
        out_specs=(whole, rows, rows, rows, rows, flat, flat),
        check_vma=False,
    )
```

```python
import jax
import jax.numpy as jnp
from jax import lax
from jax.experimental import pallas as pl
from jax.experimental.pallas import tpu as pltpu
from jax.sharding import PartitionSpec as P

HEADS = 8
HEAD_DIM = 32
D = 256
WIN = 8
HH = 32
WW = 32
FRAMES = 16
TOKENS = 1024
ROWS = 1024
SHARE = 64
GROUP = 128
HALF = 128
PACK = 4
CHUNK = 512
SPACE_STEP = 8
TIME_STEP = 4
EPSILON = 1e-06
SCALE = HEAD_DIM ** (-0.5)
F32 = jnp.float32
BF16 = jnp.bfloat16


def dot_nn(a, b):
    return lax.dot_general(a, b, (((1,), (0,)), ((), ())), preferred_element_type=F32)


def dot_nt(a, b):
    return lax.dot_general(a, b, (((1,), (1,)), ((), ())), preferred_element_type=F32)


def dot_tn(a, b):
    return lax.dot_general(a, b, (((0,), (0,)), ((), ())), preferred_element_type=F32)


def head_masks():
    lane = lax.broadcasted_iota(jnp.int32, (1, HALF), 1) // HEAD_DIM
    return [(lane == h).astype(F32).astype(BF16) for h in range(PACK)]


def spread(x, masks):
    return jnp.concatenate([x * m for m in masks], axis=0)


def spread_full(x, masks):
    low, high = spread(x[:, :HALF], masks), spread(x[:, HALF:], masks)
    zero = jnp.zeros_like(low)
    return jnp.concatenate(
        [jnp.concatenate([low, zero], axis=1), jnp.concatenate([zero, high], axis=1)], axis=0
    )


def flip_space(x):
    parts = []
    for pair in range(2):
        turned = x[:, HALF * pair : HALF * (pair + 1)].T
        parts += [turned[:SHARE], turned[SHARE:]]
    return jnp.concatenate(parts, axis=1)


def flip_time(x):
    turned = x.T
    blocks = [turned[16 * i : 16 * (i + 1)] for i in range(8)]
    lane = lax.broadcasted_iota(jnp.int32, (16, 128), 1) // 16
    for bit in range(3):
        step = 1 << bit
        upper = (lane // step) % 2 == 1
        for i in range(8):
            if not i & step:
                a, b = blocks[i], blocks[i + step]
                blocks[i] = jnp.where(upper, pltpu.roll(b, 16 * step, 1), a)
                blocks[i + step] = jnp.where(upper, b, pltpu.roll(a, 128 - 16 * step, 1))
    return blocks


def softmax_keys(scores, axis):
    scores = scores * SCALE
    ex = jnp.exp(scores - jnp.max(scores, axis=axis, keepdims=True))
    return ex * (1.0 / jnp.sum(ex, axis=axis, keepdims=True))


def score_grad(probs, dprobs, axis):
    weighted = probs * dprobs
    return weighted - probs * jnp.sum(weighted, axis=axis, keepdims=True)


def norm_factor(x):
    return lax.rsqrt(jnp.mean(x * x, -1, keepdims=True) + EPSILON)


def norm_back(dinput, normed, factor, gain):
    scaled = dinput * gain
    return factor * (scaled - normed * jnp.mean(scaled * normed, -1, keepdims=True))


def main_kernel(
    moved, gain_t, qkv_t, out_t, gain_s, qkv_s, out_s, sent,
    stage, xs, in_t, proj_t, probs_t, mixed_t, middle, in_s, proj_s, mixed_s, dmix, dproj, dmid, dmid_b,
):
    masks = head_masks()

    def rows_of(c, size=CHUNK):
        return pl.ds(pl.multiple_of(c * size, size), size)

    def strided(ref, first, count, stride):
        return jnp.concatenate(
            [ref[half, pl.ds(first, count, stride=stride), :] for half in range(2)], axis=1
        )

    def save(ref, rows, x):
        for half in range(2):
            ref[half, rows, :] = x[:, HALF * half : HALF * (half + 1)]

    def widen(f, _):
        save(stage, rows_of(f, SHARE), moved[f, :SHARE, :].astype(F32))
        return _

    lax.fori_loop(0, FRAMES, widen, 0)

    def by_token(ref, c):
        return jnp.concatenate([strided(ref, c * (CHUNK // 16) + i, FRAMES, SHARE) for i in range(CHUNK // 16)], axis=0)

    def by_frame(ref, c):
        return jnp.concatenate([strided(ref, c * (CHUNK // SHARE) + i, SHARE, FRAMES) for i in range(CHUNK // SHARE)], axis=0)

    def project_time(c, _):
        x = by_token(stage, c)
        xs[rows_of(c), :] = x
        inp = (x * norm_factor(x) * gain_t[...]).astype(BF16)
        in_t[rows_of(c), :] = inp
        proj_t[rows_of(c), :] = dot_nn(inp, qkv_t[...]).astype(BF16)
        return _

    lax.fori_loop(0, ROWS // CHUNK, project_time, 0, unroll=True)

    def token(x, s):
        return x[16 * s : 16 * (s + 1)]

    def time_forward(c, _):
        groups = [rows_of(c * TIME_STEP + i, GROUP) for i in range(TIME_STEP)]
        q, k, v = ([proj_t[rows, D * i : D * (i + 1)] for rows in groups] for i in range(3))
        qb = [[spread_full(token(x, s), masks) for s in range(8)] for x in q]
        scores = [jnp.stack([dot_nt(token(x, s), y[s]) for s in range(8)]) for x, y in zip(k, qb)]
        probs = [softmax_keys(x, 1).reshape(GROUP, 128) for x in scores]
        turned = [flip_time(x) for x in probs]
        vb = [[spread_full(token(x, s), masks) for s in range(8)] for x in v]
        mixed = [[dot_nn(x[s].astype(BF16), y[s]) for s in range(8)] for x, y in zip(turned, vb)]
        for n, rows in enumerate(groups):
            probs_t[rows, :] = probs[n].astype(BF16)
            mixed_t[rows, :] = jnp.concatenate(mixed[n], axis=0).astype(BF16)
        return _

    lax.fori_loop(0, ROWS // GROUP // TIME_STEP, time_forward, 0)

    def make_middle(c, _):
        mid = xs[rows_of(c), :] + dot_nn(mixed_t[rows_of(c), :], out_t[...])
        save(stage, rows_of(c), mid.astype(BF16).astype(F32))
        return _

    lax.fori_loop(0, ROWS // CHUNK, make_middle, 0, unroll=True)

    def cots(c):
        return moved[pl.ds(CHUNK // SHARE * c, CHUNK // SHARE), SHARE:, :].reshape(CHUNK, D)

    def project_space(c, _):
        mid = by_frame(stage, c)
        middle[rows_of(c), :] = mid
        inp = (mid * norm_factor(mid) * gain_s[...]).astype(BF16)
        in_s[rows_of(c), :] = inp
        proj_s[rows_of(c), :] = dot_nn(inp, qkv_s[...]).astype(BF16)
        dmix[rows_of(c), :] = dot_nt(cots(c), out_s[...]).astype(BF16)
        return _

    lax.fori_loop(0, ROWS // CHUNK, project_space, 0, unroll=True)

    def space(c, _):
        units = []
        for i in range(SPACE_STEP):
            rows = rows_of(c * SPACE_STEP + i, SHARE)
            units += [(rows, 0), (rows, HALF)]

        def load(ref, offset):
            return [ref[rows, offset + first : offset + first + HALF] for rows, first in units]

        q, k, v, do = load(proj_s, 0), load(proj_s, D), load(proj_s, 2 * D), load(dmix, 0)
        qb = [spread(x, masks) for x in q]
        scores = [dot_nt(x, y) for x, y in zip(k, qb)]
        dob = [spread(x, masks) for x in do]
        dprobs = [dot_nt(x, y) for x, y in zip(v, dob)]
        probs = [softmax_keys(x, 0) for x in scores]
        probs_b = [x.astype(BF16) for x in probs]
        ds = [score_grad(x, y, 0).astype(BF16) for x, y in zip(probs, dprobs)]
        turned = [flip_space(x) for x in probs_b]
        ds_turned = [flip_space(x) for x in ds]
        dv = [dot_nn(x, y) for x, y in zip(probs_b, dob)]
        dk = [dot_nn(x, y) * SCALE for x, y in zip(ds, qb)]
        mixed = [dot_nn(x, spread(y, masks)) for x, y in zip(turned, v)]
        dq = [dot_nn(x, spread(y, masks)) * SCALE for x, y in zip(ds_turned, k)]
        for n, (rows, first) in enumerate(units):
            mixed_s[rows, first : first + HALF] = mixed[n].astype(BF16)
            for i, grad in enumerate((dq, dk, dv)):
                dproj[rows, D * i + first : D * i + first + HALF] = grad[n].astype(BF16)
        return _

    lax.fori_loop(0, FRAMES // SPACE_STEP, space, 0)

    def place(first, sums):
        sums = sums.astype(BF16)
        for i in range(sums.shape[1] // D):
            for d in range(FRAMES):
                sent[d, first + 16 * i : first + 16 * (i + 1), :] = sums[
                    16 * d : 16 * (d + 1), D * i : D * (i + 1)
                ]

    place(128, dot_tn(in_s[...], dproj[...]))
    place(128 + 48, dot_tn(mixed_s[...], moved[:, SHARE:, :].reshape(ROWS, D)))

    def middle_back(c, gain_sum):
        dinput = dot_nt(dproj[rows_of(c), :], qkv_s[...])
        mid = middle[rows_of(c), :]
        factor = norm_factor(mid)
        normed = mid * factor
        save(dmid, rows_of(c), cots(c).astype(F32) + norm_back(dinput, normed, factor, gain_s[...]))
        return gain_sum + jnp.sum(dinput * normed, axis=0, keepdims=True)

    gain_sum_s = lax.fori_loop(0, ROWS // CHUNK, middle_back, jnp.zeros((1, D), F32), unroll=True)

    def mixed_back(c, _):
        dm = by_token(dmid, c).astype(BF16)
        dmid_b[rows_of(c), :] = dm
        dmix[rows_of(c), :] = dot_nt(dm, out_t[...]).astype(BF16)
        return _

    lax.fori_loop(0, ROWS // CHUNK, mixed_back, 0, unroll=True)

    def time_back(c, _):
        groups = [rows_of(c * TIME_STEP + i, GROUP) for i in range(TIME_STEP)]
        q, k, v = ([proj_t[rows, D * i : D * (i + 1)] for rows in groups] for i in range(3))
        do = [dmix[rows, :] for rows in groups]
        probs_b = [probs_t[rows, :] for rows in groups]
        tokens = range(8)
        dob = [[spread_full(token(x, s), masks) for s in tokens] for x in do]
        dprobs = [jnp.stack([dot_nt(token(x, s), y[s]) for s in tokens]) for x, y in zip(v, dob)]
        ds = [
            score_grad(x.astype(F32).reshape(8, 16, 128), y, 1).reshape(GROUP, 128)
            for x, y in zip(probs_b, dprobs)
        ]
        turned = [flip_time(x) for x in ds]
        ds = [x.astype(BF16) for x in ds]
        dv = [[dot_nn(token(x, s), y[s]) for s in tokens] for x, y in zip(probs_b, dob)]
        dk = [
            [dot_nn(token(x, s), spread_full(token(y, s), masks)) * SCALE for s in tokens]
            for x, y in zip(ds, q)
        ]
        dq = [
            [dot_nn(x[s].astype(BF16), spread_full(token(y, s), masks)) * SCALE for s in tokens]
            for x, y in zip(turned, k)
        ]
        for n, rows in enumerate(groups):
            for i, grad in enumerate((dq, dk, dv)):
                dproj[rows, D * i : D * (i + 1)] = jnp.concatenate(grad[n], axis=0).astype(BF16)
        return _

    lax.fori_loop(0, ROWS // GROUP // TIME_STEP, time_back, 0)

    place(64, dot_tn(in_t[...], dproj[...]))
    place(64 + 48, dot_tn(mixed_t[...], dmid_b[...]))

    def input_back(c, gain_sum):
        dinput = dot_nt(dproj[rows_of(c), :], qkv_t[...])
        x = xs[rows_of(c), :]
        factor = norm_factor(x)
        normed = x * factor
        save(stage, rows_of(c), norm_back(dinput, normed, factor, gain_t[...]))
        return gain_sum + jnp.sum(dinput * normed, axis=0, keepdims=True)

    gain_sum_t = lax.fori_loop(0, ROWS // CHUNK, input_back, jnp.zeros((1, D), F32), unroll=True)

    gains = jnp.concatenate([gain_sum_t, gain_sum_s], axis=0)
    high = gains.astype(BF16).astype(F32)
    low = gains - high
    extra = jnp.concatenate([high, low, jnp.zeros((12, D), F32)], axis=0).astype(BF16)

    def restore(f, _):
        for half in range(2):
            dnorm = stage[half, pl.ds(f, SHARE, stride=FRAMES), :]
            total = dmid[half, rows_of(f, SHARE), :] + dnorm
            sent[f, :SHARE, HALF * half : HALF * (half + 1)] = total.astype(BF16)
        sent[f, 192:208, :] = extra
        return _

    lax.fori_loop(0, FRAMES, restore, 0)


def run_main(moved, gain_t, qkv_t, out_t, gain_s, qkv_s, out_s):
    def rows(width, kind):
        return pltpu.VMEM((ROWS, width), kind)

    return pl.pallas_call(
        main_kernel,
        out_shape=jax.ShapeDtypeStruct((FRAMES, 208, D), BF16),
        scratch_shapes=[
            pltpu.VMEM((2, ROWS, HALF), F32),
            rows(D, F32),
            rows(D, BF16),
            rows(3 * D, BF16),
            rows(128, BF16),
            rows(D, BF16),
            rows(D, F32),
            rows(D, BF16),
            rows(3 * D, BF16),
            rows(D, BF16),
            rows(D, BF16),
            rows(3 * D, BF16),
            pltpu.VMEM((2, ROWS, HALF), F32),
            rows(D, BF16),
        ],
        compiler_params=pltpu.CompilerParams(vmem_limit_bytes=40 * 1024 * 1024),
        cost_estimate=pl.CostEstimate(
            flops=8 * 10**9, bytes_accessed=6 * 10**6, transcendentals=2 * 10**6
        ),
    )(moved, gain_t.reshape(1, D), qkv_t, out_t, gain_s.reshape(1, D), qkv_s, out_s)


def to_windows(frame):
    split = frame.reshape(HH // WIN, WIN, WW // WIN, WIN, D)
    return split.transpose(0, 2, 1, 3, 4).reshape(FRAMES, SHARE, D)


def from_windows(windows):
    split = windows.reshape(HH // WIN, WW // WIN, WIN, WIN, D)
    return split.transpose(0, 2, 1, 3, 4).reshape(1, TOKENS, D)


def exchange(x):
    return lax.all_to_all(x, "frame", split_axis=0, concat_axis=0, tiled=True)


def per_device(latents, cotangent, gain_time, qkv_time, out_time, gain_space, qkv_space, out_space):
    moved = exchange(jnp.concatenate([to_windows(latents), to_windows(cotangent)], axis=1))
    sent = run_main(moved, gain_time, qkv_time, out_time, gain_space, qkv_space, out_space)
    back = exchange(sent).astype(F32)
    grad_latents = from_windows(back[:, :SHARE])
    inverse = 1.0 / jnp.sqrt(jnp.float32(FRAMES * TOKENS))
    sums = jnp.sum(back[:, SHARE:], axis=0) * inverse

    def weights(first):
        qkv = jnp.concatenate([sums[first + 16 * i : first + 16 * (i + 1)] for i in range(3)], axis=1)
        return qkv, sums[first + 48 : first + 64]

    qkv_t, out_t = weights(0)
    qkv_s, out_s = weights(64)
    mine = lax.axis_index("frame") * 16
    gains = lax.dynamic_slice_in_dim(sums[128:130] + sums[130:132], mine, 16, axis=1)
    return (grad_latents, qkv_t, out_t, qkv_s, out_s, gains[0], gains[1])


def solution(mesh):
    whole = P(("dp", "frame"), None, None)
    rows = P(("dp", "frame"), None)
    flat = P(("dp", "frame"))
    return jax.shard_map(
        per_device,
        mesh=mesh,
        in_specs=(whole, whole, P(), P(), P(), P(), P(), P()),
        out_specs=(whole, rows, rows, rows, rows, flat, flat),
        check_vma=False,
    )
```

```python
import jax
import jax.numpy as jnp
from jax import lax
from jax.experimental import pallas as pl
from jax.experimental.pallas import tpu as pltpu
from jax.sharding import PartitionSpec as P

HEADS = 8
HEAD_DIM = 32
D = 256
WIN = 8
HH = 32
WW = 32
FRAMES = 16
TOKENS = 1024
ROWS = 1024
SHARE = 64
GROUP = 128
HALF = 128
PACK = 4
CHUNK = 512
SPACE_STEP = 16
TIME_STEP = 8
EPSILON = 1e-06
SCALE = HEAD_DIM ** (-0.5)
F32 = jnp.float32
BF16 = jnp.bfloat16


def dot_nn(a, b):
    return lax.dot_general(a, b, (((1,), (0,)), ((), ())), preferred_element_type=F32)


def dot_nt(a, b):
    return lax.dot_general(a, b, (((1,), (1,)), ((), ())), preferred_element_type=F32)


def dot_tn(a, b):
    return lax.dot_general(a, b, (((0,), (0,)), ((), ())), preferred_element_type=F32)


def head_masks():
    lane = lax.broadcasted_iota(jnp.int32, (1, HALF), 1) // HEAD_DIM
    return [(lane == h).astype(F32).astype(BF16) for h in range(PACK)]


def spread(x, masks):
    return jnp.concatenate([x * m for m in masks], axis=0)


def spread_full(x, masks):
    low, high = spread(x[:, :HALF], masks), spread(x[:, HALF:], masks)
    zero = jnp.zeros_like(low)
    return jnp.concatenate(
        [jnp.concatenate([low, zero], axis=1), jnp.concatenate([zero, high], axis=1)], axis=0
    )


def flip_space(x):
    parts = []
    for pair in range(2):
        turned = x[:, HALF * pair : HALF * (pair + 1)].T
        parts += [turned[:SHARE], turned[SHARE:]]
    return jnp.concatenate(parts, axis=1)


def flip_time(x):
    turned = x.T
    blocks = [turned[16 * i : 16 * (i + 1)] for i in range(8)]
    lane = lax.broadcasted_iota(jnp.int32, (16, 128), 1) // 16
    for bit in range(3):
        step = 1 << bit
        upper = (lane // step) % 2 == 1
        for i in range(8):
            if not i & step:
                a, b = blocks[i], blocks[i + step]
                blocks[i] = jnp.where(upper, pltpu.roll(b, 16 * step, 1), a)
                blocks[i + step] = jnp.where(upper, b, pltpu.roll(a, 128 - 16 * step, 1))
    return blocks


def softmax_keys(scores, axis):
    scores = scores * SCALE
    ex = jnp.exp(scores - jnp.max(scores, axis=axis, keepdims=True))
    return ex * (1.0 / jnp.sum(ex, axis=axis, keepdims=True))


def score_grad(probs, dprobs, axis):
    weighted = probs * dprobs
    return weighted - probs * jnp.sum(weighted, axis=axis, keepdims=True)


def norm_factor(x):
    return lax.rsqrt(jnp.mean(x * x, -1, keepdims=True) + EPSILON)


def norm_back(dinput, normed, factor, gain):
    scaled = dinput * gain
    return factor * (scaled - normed * jnp.mean(scaled * normed, -1, keepdims=True))


def main_kernel(
    moved, gain_t, qkv_t, out_t, gain_s, qkv_s, out_s, sent,
    stage, xs, in_t, proj_t, probs_t, mixed_t, middle, in_s, proj_s, mixed_s, dmix, dproj, dmid, dmid_b,
):
    masks = head_masks()

    def rows_of(c, size=CHUNK):
        return pl.ds(pl.multiple_of(c * size, size), size)

    def strided(ref, first, count, stride):
        return jnp.concatenate(
            [ref[half, pl.ds(first, count, stride=stride), :] for half in range(2)], axis=1
        )

    def save(ref, rows, x):
        for half in range(2):
            ref[half, rows, :] = x[:, HALF * half : HALF * (half + 1)]

    def widen(f, _):
        save(stage, rows_of(f, SHARE), moved[f, :SHARE, :].astype(F32))
        return _

    lax.fori_loop(0, FRAMES, widen, 0)

    def by_token(ref, c):
        return jnp.concatenate([strided(ref, c * (CHUNK // 16) + i, FRAMES, SHARE) for i in range(CHUNK // 16)], axis=0)

    def by_frame(ref, c):
        return jnp.concatenate([strided(ref, c * (CHUNK // SHARE) + i, SHARE, FRAMES) for i in range(CHUNK // SHARE)], axis=0)

    def project_time(c, _):
        x = by_token(stage, c)
        xs[rows_of(c), :] = x
        inp = (x * norm_factor(x) * gain_t[...]).astype(BF16)
        in_t[rows_of(c), :] = inp
        proj_t[rows_of(c), :] = dot_nn(inp, qkv_t[...]).astype(BF16)
        return _

    lax.fori_loop(0, ROWS // CHUNK, project_time, 0, unroll=True)

    def token(x, s):
        return x[16 * s : 16 * (s + 1)]

    def time_forward(c, _):
        groups = [rows_of(c * TIME_STEP + i, GROUP) for i in range(TIME_STEP)]
        q, k, v = ([proj_t[rows, D * i : D * (i + 1)] for rows in groups] for i in range(3))
        qb = [[spread_full(token(x, s), masks) for s in range(8)] for x in q]
        scores = [jnp.stack([dot_nt(token(x, s), y[s]) for s in range(8)]) for x, y in zip(k, qb)]
        probs = [softmax_keys(x, 1).reshape(GROUP, 128) for x in scores]
        turned = [flip_time(x) for x in probs]
        vb = [[spread_full(token(x, s), masks) for s in range(8)] for x in v]
        mixed = [[dot_nn(x[s].astype(BF16), y[s]) for s in range(8)] for x, y in zip(turned, vb)]
        for n, rows in enumerate(groups):
            probs_t[rows, :] = probs[n].astype(BF16)
            mixed_t[rows, :] = jnp.concatenate(mixed[n], axis=0).astype(BF16)
        return _

    lax.fori_loop(0, ROWS // GROUP // TIME_STEP, time_forward, 0)

    def make_middle(c, _):
        mid = xs[rows_of(c), :] + dot_nn(mixed_t[rows_of(c), :], out_t[...])
        save(stage, rows_of(c), mid.astype(BF16).astype(F32))
        return _

    lax.fori_loop(0, ROWS // CHUNK, make_middle, 0, unroll=True)

    def cots(c):
        return moved[pl.ds(CHUNK // SHARE * c, CHUNK // SHARE), SHARE:, :].reshape(CHUNK, D)

    def project_space(c, _):
        mid = by_frame(stage, c)
        middle[rows_of(c), :] = mid
        inp = (mid * norm_factor(mid) * gain_s[...]).astype(BF16)
        in_s[rows_of(c), :] = inp
        proj_s[rows_of(c), :] = dot_nn(inp, qkv_s[...]).astype(BF16)
        dmix[rows_of(c), :] = dot_nt(cots(c), out_s[...]).astype(BF16)
        return _

    lax.fori_loop(0, ROWS // CHUNK, project_space, 0, unroll=True)

    def space(c, _):
        units = []
        for i in range(SPACE_STEP):
            rows = rows_of(c * SPACE_STEP + i, SHARE)
            units += [(rows, 0), (rows, HALF)]

        def load(ref, offset):
            return [ref[rows, offset + first : offset + first + HALF] for rows, first in units]

        q, k, v, do = load(proj_s, 0), load(proj_s, D), load(proj_s, 2 * D), load(dmix, 0)
        qb = [spread(x, masks) for x in q]
        scores = [dot_nt(x, y) for x, y in zip(k, qb)]
        dob = [spread(x, masks) for x in do]
        dprobs = [dot_nt(x, y) for x, y in zip(v, dob)]
        probs = [softmax_keys(x, 0) for x in scores]
        probs_b = [x.astype(BF16) for x in probs]
        ds = [score_grad(x, y, 0).astype(BF16) for x, y in zip(probs, dprobs)]
        turned = [flip_space(x) for x in probs_b]
        ds_turned = [flip_space(x) for x in ds]
        dv = [dot_nn(x, y) for x, y in zip(probs_b, dob)]
        dk = [dot_nn(x, y) * SCALE for x, y in zip(ds, qb)]
        mixed = [dot_nn(x, spread(y, masks)) for x, y in zip(turned, v)]
        dq = [dot_nn(x, spread(y, masks)) * SCALE for x, y in zip(ds_turned, k)]
        for n, (rows, first) in enumerate(units):
            mixed_s[rows, first : first + HALF] = mixed[n].astype(BF16)
            for i, grad in enumerate((dq, dk, dv)):
                dproj[rows, D * i + first : D * i + first + HALF] = grad[n].astype(BF16)
        return _

    lax.fori_loop(0, FRAMES // SPACE_STEP, space, 0)

    def place(first, sums):
        sums = sums.astype(BF16)
        for i in range(sums.shape[1] // D):
            for d in range(FRAMES):
                sent[d, first + 16 * i : first + 16 * (i + 1), :] = sums[
                    16 * d : 16 * (d + 1), D * i : D * (i + 1)
                ]

    place(128, dot_tn(in_s[...], dproj[...]))
    place(128 + 48, dot_tn(mixed_s[...], moved[:, SHARE:, :].reshape(ROWS, D)))

    def middle_back(c, gain_sum):
        dinput = dot_nt(dproj[rows_of(c), :], qkv_s[...])
        mid = middle[rows_of(c), :]
        factor = norm_factor(mid)
        normed = mid * factor
        save(dmid, rows_of(c), cots(c).astype(F32) + norm_back(dinput, normed, factor, gain_s[...]))
        return gain_sum + jnp.sum(dinput * normed, axis=0, keepdims=True)

    gain_sum_s = lax.fori_loop(0, ROWS // CHUNK, middle_back, jnp.zeros((1, D), F32), unroll=True)

    def mixed_back(c, _):
        dm = by_token(dmid, c).astype(BF16)
        dmid_b[rows_of(c), :] = dm
        dmix[rows_of(c), :] = dot_nt(dm, out_t[...]).astype(BF16)
        return _

    lax.fori_loop(0, ROWS // CHUNK, mixed_back, 0, unroll=True)

    def time_back(c, _):
        groups = [rows_of(c * TIME_STEP + i, GROUP) for i in range(TIME_STEP)]
        q, k, v = ([proj_t[rows, D * i : D * (i + 1)] for rows in groups] for i in range(3))
        do = [dmix[rows, :] for rows in groups]
        probs_b = [probs_t[rows, :] for rows in groups]
        tokens = range(8)
        dob = [[spread_full(token(x, s), masks) for s in tokens] for x in do]
        dprobs = [jnp.stack([dot_nt(token(x, s), y[s]) for s in tokens]) for x, y in zip(v, dob)]
        ds = [
            score_grad(x.astype(F32).reshape(8, 16, 128), y, 1).reshape(GROUP, 128)
            for x, y in zip(probs_b, dprobs)
        ]
        turned = [flip_time(x) for x in ds]
        ds = [x.astype(BF16) for x in ds]
        dv = [[dot_nn(token(x, s), y[s]) for s in tokens] for x, y in zip(probs_b, dob)]
        dk = [
            [dot_nn(token(x, s), spread_full(token(y, s), masks)) * SCALE for s in tokens]
            for x, y in zip(ds, q)
        ]
        dq = [
            [dot_nn(x[s].astype(BF16), spread_full(token(y, s), masks)) * SCALE for s in tokens]
            for x, y in zip(turned, k)
        ]
        for n, rows in enumerate(groups):
            for i, grad in enumerate((dq, dk, dv)):
                dproj[rows, D * i : D * (i + 1)] = jnp.concatenate(grad[n], axis=0).astype(BF16)
        return _

    lax.fori_loop(0, ROWS // GROUP // TIME_STEP, time_back, 0)

    place(64, dot_tn(in_t[...], dproj[...]))
    place(64 + 48, dot_tn(mixed_t[...], dmid_b[...]))

    def input_back(c, gain_sum):
        dinput = dot_nt(dproj[rows_of(c), :], qkv_t[...])
        x = xs[rows_of(c), :]
        factor = norm_factor(x)
        normed = x * factor
        save(stage, rows_of(c), norm_back(dinput, normed, factor, gain_t[...]))
        return gain_sum + jnp.sum(dinput * normed, axis=0, keepdims=True)

    gain_sum_t = lax.fori_loop(0, ROWS // CHUNK, input_back, jnp.zeros((1, D), F32), unroll=True)

    gains = jnp.concatenate([gain_sum_t, gain_sum_s], axis=0)
    high = gains.astype(BF16).astype(F32)
    low = gains - high
    extra = jnp.concatenate([high, low, jnp.zeros((12, D), F32)], axis=0)
    for d in range(FRAMES):
        turned = extra if d == 0 else pltpu.roll(extra, D - 16 * d, 1)
        sent[d, 192:208, :] = turned.astype(BF16)

    def restore(f, _):
        for half in range(2):
            dnorm = stage[half, pl.ds(f, SHARE, stride=FRAMES), :]
            total = dmid[half, rows_of(f, SHARE), :] + dnorm
            sent[f, :SHARE, HALF * half : HALF * (half + 1)] = total.astype(BF16)
        return _

    lax.fori_loop(0, FRAMES, restore, 0)


def run_main(moved, gain_t, qkv_t, out_t, gain_s, qkv_s, out_s):
    def rows(width, kind):
        return pltpu.VMEM((ROWS, width), kind)

    return pl.pallas_call(
        main_kernel,
        out_shape=jax.ShapeDtypeStruct((FRAMES, 208, D), BF16),
        scratch_shapes=[
            pltpu.VMEM((2, ROWS, HALF), F32),
            rows(D, F32),
            rows(D, BF16),
            rows(3 * D, BF16),
            rows(128, BF16),
            rows(D, BF16),
            rows(D, F32),
            rows(D, BF16),
            rows(3 * D, BF16),
            rows(D, BF16),
            rows(D, BF16),
            rows(3 * D, BF16),
            pltpu.VMEM((2, ROWS, HALF), F32),
            rows(D, BF16),
        ],
        compiler_params=pltpu.CompilerParams(vmem_limit_bytes=40 * 1024 * 1024),
        cost_estimate=pl.CostEstimate(
            flops=8 * 10**9, bytes_accessed=6 * 10**6, transcendentals=2 * 10**6
        ),
    )(moved, gain_t.reshape(1, D), qkv_t, out_t, gain_s.reshape(1, D), qkv_s, out_s)


def pack_kernel(latents, cotangent, packed):
    for wy in range(4):
        for pair in range(4):
            first = 64 * (4 * wy + pair)
            for src, base in ((latents, 0), (cotangent, SHARE)):
                rows = src[0, first : first + 64, :].astype(F32).reshape(2, 4, WIN, D)
                for wx in range(4):
                    both = jnp.concatenate([rows[0, wx], rows[1, wx]], axis=0).astype(BF16)
                    packed[4 * wy + wx, base + 16 * pair : base + 16 * (pair + 1), :] = both


def pack(latents, cotangent):
    return pl.pallas_call(
        pack_kernel,
        out_shape=jax.ShapeDtypeStruct((FRAMES, 2 * SHARE, D), BF16),
    )(latents, cotangent)


def unpack_kernel(back, grads, qkv_t, out_t, qkv_s, out_s, gains):
    for wy in range(4):
        for pair in range(4):
            rows = back[4 * wy : 4 * wy + 4, 16 * pair : 16 * (pair + 1), :].astype(F32)
            first = 64 * (4 * wy + pair)
            for wx in range(4):
                for i in range(2):
                    start = first + 32 * i + WIN * wx
                    grads[0, start : start + WIN, :] = rows[wx, WIN * i : WIN * (i + 1)]
    inverse = (FRAMES * TOKENS) ** (-0.5)

    def total(first):
        return jnp.sum(back[:, first : first + 16, :].astype(F32), axis=0) * inverse

    for first, qkv, out in ((SHARE, qkv_t, out_t), (2 * SHARE, qkv_s, out_s)):
        for i in range(3):
            qkv[:, D * i : D * (i + 1)] = total(first + 16 * i)
        out[...] = total(first + 48)
    sums = total(192)
    gains[...] = sums[0:2, :128] + sums[2:4, :128]


def unpack(back):
    def out(*shape):
        return jax.ShapeDtypeStruct(shape, F32)

    return pl.pallas_call(
        unpack_kernel,
        out_shape=(
            out(1, TOKENS, D), out(16, 3 * D), out(16, D), out(16, 3 * D), out(16, D), out(2, 128)
        ),
    )(back)


def exchange(x):
    return lax.all_to_all(x, "frame", split_axis=0, concat_axis=0, tiled=True)


def per_device(latents, cotangent, gain_time, qkv_time, out_time, gain_space, qkv_space, out_space):
    moved = exchange(pack(latents, cotangent))
    sent = run_main(moved, gain_time, qkv_time, out_time, gain_space, qkv_space, out_space)
    *grads, gains = unpack(exchange(sent))
    return (*grads, gains[0, :16], gains[1, :16])


def solution(mesh):
    whole = P(("dp", "frame"), None, None)
    rows = P(("dp", "frame"), None)
    flat = P(("dp", "frame"))
    return jax.shard_map(
        per_device,
        mesh=mesh,
        in_specs=(whole, whole, P(), P(), P(), P(), P(), P()),
        out_specs=(whole, rows, rows, rows, rows, flat, flat),
        check_vma=False,
    )
```

```python
import jax
import jax.numpy as jnp
from jax import lax
from jax.experimental import pallas as pl
from jax.experimental.pallas import tpu as pltpu
from jax.sharding import PartitionSpec as P

HEADS = 8
HEAD_DIM = 32
D = 256
WIN = 8
HH = 32
WW = 32
FRAMES = 16
TOKENS = 1024
ROWS = 1024
SHARE = 64
GROUP = 128
HALF = 128
PACK = 4
CHUNK = 512
SPACE_STEP = 16
TIME_STEP = 8
EPSILON = 1e-06
SCALE = HEAD_DIM ** (-0.5)
F32 = jnp.float32
BF16 = jnp.bfloat16


def dot_nn(a, b):
    return lax.dot_general(a, b, (((1,), (0,)), ((), ())), preferred_element_type=F32)


def dot_nt(a, b):
    return lax.dot_general(a, b, (((1,), (1,)), ((), ())), preferred_element_type=F32)


def dot_tn(a, b):
    return lax.dot_general(a, b, (((0,), (0,)), ((), ())), preferred_element_type=F32)


def head_masks():
    lane = lax.broadcasted_iota(jnp.int32, (1, HALF), 1) // HEAD_DIM
    return [(lane == h).astype(F32).astype(BF16) for h in range(PACK)]


def spread(x, masks):
    return jnp.concatenate([x * m for m in masks], axis=0)


def spread_full(x, masks):
    low, high = spread(x[:, :HALF], masks), spread(x[:, HALF:], masks)
    zero = jnp.zeros_like(low)
    return jnp.concatenate(
        [jnp.concatenate([low, zero], axis=1), jnp.concatenate([zero, high], axis=1)], axis=0
    )


def flip_space(x):
    parts = []
    for pair in range(2):
        turned = x[:, HALF * pair : HALF * (pair + 1)].T
        parts += [turned[:SHARE], turned[SHARE:]]
    return jnp.concatenate(parts, axis=1)


def flip_time(x):
    turned = x.T
    blocks = [turned[16 * i : 16 * (i + 1)] for i in range(8)]
    lane = lax.broadcasted_iota(jnp.int32, (16, 128), 1) // 16
    for bit in range(3):
        step = 1 << bit
        upper = (lane // step) % 2 == 1
        for i in range(8):
            if not i & step:
                a, b = blocks[i], blocks[i + step]
                blocks[i] = jnp.where(upper, pltpu.roll(b, 16 * step, 1), a)
                blocks[i + step] = jnp.where(upper, b, pltpu.roll(a, 128 - 16 * step, 1))
    return blocks


def softmax_keys(scores, axis):
    scores = scores * SCALE
    ex = jnp.exp(scores - jnp.max(scores, axis=axis, keepdims=True))
    return ex * (1.0 / jnp.sum(ex, axis=axis, keepdims=True))


def score_grad(probs, dprobs, axis):
    weighted = probs * dprobs
    return weighted - probs * jnp.sum(weighted, axis=axis, keepdims=True)


def norm_factor(x):
    return lax.rsqrt(jnp.mean(x * x, -1, keepdims=True) + EPSILON)


def norm_back(dinput, normed, factor, gain):
    scaled = dinput * gain
    return factor * (scaled - normed * jnp.mean(scaled * normed, -1, keepdims=True))


def rows_of(c, size=CHUNK):
    return pl.ds(pl.multiple_of(c * size, size), size)


def save(ref, rows, x):
    for half in range(2):
        ref[half, rows, :] = x[:, HALF * half : HALF * (half + 1)]


def main_kernel(
    moved, gain_t, qkv_t, out_t, gain_s, qkv_s, out_s, xs, dproj, dmid, gain_sum_s, kept, given,
    stage, in_t, proj_t, probs_t, mixed_t, middle, in_s, proj_s, mixed_s, dmix, dmid_b, parts,
):
    masks = head_masks()

    def strided(ref, first, count, stride):
        return jnp.concatenate(
            [ref[half, pl.ds(first, count, stride=stride), :] for half in range(2)], axis=1
        )

    def widen(f, _):
        save(stage, rows_of(f, SHARE), moved[f, :SHARE, :].astype(F32))
        return _

    lax.fori_loop(0, FRAMES, widen, 0)

    def by_token(ref, c):
        return jnp.concatenate([strided(ref, c * (CHUNK // 16) + i, FRAMES, SHARE) for i in range(CHUNK // 16)], axis=0)

    def by_frame(ref, c):
        return jnp.concatenate([strided(ref, c * (CHUNK // SHARE) + i, SHARE, FRAMES) for i in range(CHUNK // SHARE)], axis=0)

    def project_time(c, _):
        x = by_token(stage, c)
        xs[rows_of(c), :] = x
        inp = (x * norm_factor(x) * gain_t[...]).astype(BF16)
        in_t[rows_of(c), :] = inp
        proj_t[rows_of(c), :] = dot_nn(inp, qkv_t[...]).astype(BF16)
        return _

    lax.fori_loop(0, ROWS // CHUNK, project_time, 0, unroll=True)

    def token(x, s):
        return x[16 * s : 16 * (s + 1)]

    def time_forward(c, _):
        groups = [rows_of(c * TIME_STEP + i, GROUP) for i in range(TIME_STEP)]
        q, k, v = ([proj_t[rows, D * i : D * (i + 1)] for rows in groups] for i in range(3))
        qb = [[spread_full(token(x, s), masks) for s in range(8)] for x in q]
        scores = [jnp.stack([dot_nt(token(x, s), y[s]) for s in range(8)]) for x, y in zip(k, qb)]
        probs = [softmax_keys(x, 1).reshape(GROUP, 128) for x in scores]
        turned = [flip_time(x) for x in probs]
        vb = [[spread_full(token(x, s), masks) for s in range(8)] for x in v]
        mixed = [[dot_nn(x[s].astype(BF16), y[s]) for s in range(8)] for x, y in zip(turned, vb)]
        for n, rows in enumerate(groups):
            probs_t[rows, :] = probs[n].astype(BF16)
            mixed_t[rows, :] = jnp.concatenate(mixed[n], axis=0).astype(BF16)
        return _

    lax.fori_loop(0, ROWS // GROUP // TIME_STEP, time_forward, 0)

    def make_middle(c, _):
        mid = xs[rows_of(c), :] + dot_nn(mixed_t[rows_of(c), :], out_t[...])
        save(stage, rows_of(c), mid.astype(BF16).astype(F32))
        return _

    lax.fori_loop(0, ROWS // CHUNK, make_middle, 0, unroll=True)

    def cots(c):
        return moved[pl.ds(CHUNK // SHARE * c, CHUNK // SHARE), SHARE:, :].reshape(CHUNK, D)

    def project_space(c, _):
        mid = by_frame(stage, c)
        middle[rows_of(c), :] = mid
        inp = (mid * norm_factor(mid) * gain_s[...]).astype(BF16)
        in_s[rows_of(c), :] = inp
        proj_s[rows_of(c), :] = dot_nn(inp, qkv_s[...]).astype(BF16)
        dmix[rows_of(c), :] = dot_nt(cots(c), out_s[...]).astype(BF16)
        return _

    lax.fori_loop(0, ROWS // CHUNK, project_space, 0, unroll=True)

    def space(c, _):
        units = []
        for i in range(SPACE_STEP):
            rows = rows_of(c * SPACE_STEP + i, SHARE)
            units += [(rows, 0), (rows, HALF)]

        def load(ref, offset):
            return [ref[rows, offset + first : offset + first + HALF] for rows, first in units]

        q, k, v, do = load(proj_s, 0), load(proj_s, D), load(proj_s, 2 * D), load(dmix, 0)
        qb = [spread(x, masks) for x in q]
        scores = [dot_nt(x, y) for x, y in zip(k, qb)]
        dob = [spread(x, masks) for x in do]
        dprobs = [dot_nt(x, y) for x, y in zip(v, dob)]
        probs = [softmax_keys(x, 0) for x in scores]
        probs_b = [x.astype(BF16) for x in probs]
        ds = [score_grad(x, y, 0).astype(BF16) for x, y in zip(probs, dprobs)]
        turned = [flip_space(x) for x in probs_b]
        ds_turned = [flip_space(x) for x in ds]
        dv = [dot_nn(x, y) for x, y in zip(probs_b, dob)]
        dk = [dot_nn(x, y) * SCALE for x, y in zip(ds, qb)]
        mixed = [dot_nn(x, spread(y, masks)) for x, y in zip(turned, v)]
        dq = [dot_nn(x, spread(y, masks)) * SCALE for x, y in zip(ds_turned, k)]
        for n, (rows, first) in enumerate(units):
            mixed_s[rows, first : first + HALF] = mixed[n].astype(BF16)
            for i, grad in enumerate((dq, dk, dv)):
                dproj[rows, D * i + first : D * i + first + HALF] = grad[n].astype(BF16)
        return _

    lax.fori_loop(0, FRAMES // SPACE_STEP, space, 0)

    def place(kind, first, sums):
        sums = sums.astype(BF16)
        for i in range(sums.shape[1] // D):
            for d in range(FRAMES):
                parts[kind, d, first + 16 * i : first + 16 * (i + 1), :] = sums[
                    16 * d : 16 * (d + 1), D * i : D * (i + 1)
                ]

    place(1, 0, dot_tn(in_s[...], dproj[...]))
    place(1, 48, dot_tn(mixed_s[...], moved[:, SHARE:, :].reshape(ROWS, D)))

    def middle_back(c, gain_sum):
        dinput = dot_nt(dproj[rows_of(c), :], qkv_s[...])
        mid = middle[rows_of(c), :]
        factor = norm_factor(mid)
        normed = mid * factor
        save(dmid, rows_of(c), cots(c).astype(F32) + norm_back(dinput, normed, factor, gain_s[...]))
        return gain_sum + jnp.sum(dinput * normed, axis=0, keepdims=True)

    gain_sum_s[...] = lax.fori_loop(0, ROWS // CHUNK, middle_back, jnp.zeros((1, D), F32), unroll=True)

    def mixed_back(c, _):
        dm = by_token(dmid, c).astype(BF16)
        dmid_b[rows_of(c), :] = dm
        dmix[rows_of(c), :] = dot_nt(dm, out_t[...]).astype(BF16)
        return _

    lax.fori_loop(0, ROWS // CHUNK, mixed_back, 0, unroll=True)

    def time_back(c, _):
        groups = [rows_of(c * TIME_STEP + i, GROUP) for i in range(TIME_STEP)]
        q, k, v = ([proj_t[rows, D * i : D * (i + 1)] for rows in groups] for i in range(3))
        do = [dmix[rows, :] for rows in groups]
        probs_b = [probs_t[rows, :] for rows in groups]
        tokens = range(8)
        dob = [[spread_full(token(x, s), masks) for s in tokens] for x in do]
        dprobs = [jnp.stack([dot_nt(token(x, s), y[s]) for s in tokens]) for x, y in zip(v, dob)]
        ds = [
            score_grad(x.astype(F32).reshape(8, 16, 128), y, 1).reshape(GROUP, 128)
            for x, y in zip(probs_b, dprobs)
        ]
        turned = [flip_time(x) for x in ds]
        ds = [x.astype(BF16) for x in ds]
        dv = [[dot_nn(token(x, s), y[s]) for s in tokens] for x, y in zip(probs_b, dob)]
        dk = [
            [dot_nn(token(x, s), spread_full(token(y, s), masks)) * SCALE for s in tokens]
            for x, y in zip(ds, q)
        ]
        dq = [
            [dot_nn(x[s].astype(BF16), spread_full(token(y, s), masks)) * SCALE for s in tokens]
            for x, y in zip(turned, k)
        ]
        for n, rows in enumerate(groups):
            for i, grad in enumerate((dq, dk, dv)):
                dproj[rows, D * i : D * (i + 1)] = jnp.concatenate(grad[n], axis=0).astype(BF16)
        return _

    lax.fori_loop(0, ROWS // GROUP // TIME_STEP, time_back, 0)

    place(0, 0, dot_tn(in_t[...], dproj[...]))
    place(0, 48, dot_tn(mixed_t[...], dmid_b[...]))

    core = lax.axis_index("frame") % 2
    kept[...] = parts[core]
    given[...] = parts[1 - core]


def input_kernel(xs, dproj, dmid, gain_sum_s, gain_t, qkv_t, sent, stage):
    def input_back(c, gain_sum):
        dinput = dot_nt(dproj[rows_of(c), :], qkv_t[...])
        x = xs[rows_of(c), :]
        factor = norm_factor(x)
        normed = x * factor
        save(stage, rows_of(c), norm_back(dinput, normed, factor, gain_t[...]))
        return gain_sum + jnp.sum(dinput * normed, axis=0, keepdims=True)

    gain_sum_t = lax.fori_loop(0, ROWS // CHUNK, input_back, jnp.zeros((1, D), F32), unroll=True)

    gains = jnp.concatenate([gain_sum_t, gain_sum_s[...]], axis=0)
    high = gains.astype(BF16).astype(F32)
    low = gains - high
    extra = jnp.concatenate([high, low, jnp.zeros((12, D), F32)], axis=0)
    for f in range(FRAMES):
        turned = extra if f == 0 else pltpu.roll(extra, D - 16 * f, 1)
        sent[f, SHARE:, :] = turned.astype(BF16)
        for half in range(2):
            dnorm = stage[half, pl.ds(f, SHARE, stride=FRAMES), :]
            total = dmid[half, SHARE * f : SHARE * (f + 1), :] + dnorm
            sent[f, :SHARE, HALF * half : HALF * (half + 1)] = total.astype(BF16)


def join_kernel(grads, kept, taken, sent):
    sent[:, : SHARE + 16, :] = grads[...]
    sent[:, SHARE + 16 :, :] = (kept[...].astype(F32) + taken[...].astype(F32)).astype(BF16)


def shaped(kind, *shape):
    return jax.ShapeDtypeStruct(shape, kind)


def params(mebibytes):
    return pltpu.CompilerParams(vmem_limit_bytes=mebibytes * 1024 * 1024)


def run_main(moved, gain_t, qkv_t, out_t, gain_s, qkv_s, out_s):
    def rows(width, kind):
        return pltpu.VMEM((ROWS, width), kind)

    return pl.pallas_call(
        main_kernel,
        out_shape=(
            shaped(F32, ROWS, D),
            shaped(BF16, ROWS, 3 * D),
            shaped(F32, 2, ROWS, HALF),
            shaped(F32, 1, D),
            shaped(BF16, FRAMES, SHARE, D),
            shaped(BF16, FRAMES, SHARE, D),
        ),
        scratch_shapes=[
            pltpu.VMEM((2, ROWS, HALF), F32),
            rows(D, BF16),
            rows(3 * D, BF16),
            rows(128, BF16),
            rows(D, BF16),
            rows(D, F32),
            rows(D, BF16),
            rows(3 * D, BF16),
            rows(D, BF16),
            rows(D, BF16),
            rows(D, BF16),
            pltpu.VMEM((2, FRAMES, SHARE, D), BF16),
        ],
        compiler_params=params(40),
        cost_estimate=pl.CostEstimate(
            flops=8 * 10**9, bytes_accessed=6 * 10**6, transcendentals=2 * 10**6
        ),
    )(moved, gain_t, qkv_t, out_t, gain_s, qkv_s, out_s)


def run_input(xs, dproj, dmid, gain_sum_s, gain_t, qkv_t):
    return pl.pallas_call(
        input_kernel,
        out_shape=shaped(BF16, FRAMES, SHARE + 16, D),
        scratch_shapes=[pltpu.VMEM((2, ROWS, HALF), F32)],
        compiler_params=params(16),
        cost_estimate=pl.CostEstimate(flops=2 * 10**9, bytes_accessed=6 * 10**6, transcendentals=0),
    )(xs, dproj, dmid, gain_sum_s, gain_t, qkv_t)


def join(grads, kept, taken):
    return pl.pallas_call(
        join_kernel,
        out_shape=shaped(BF16, FRAMES, 2 * SHARE + 16, D),
        compiler_params=params(8),
    )(grads, kept, taken)


def pack_kernel(latents, cotangent, packed, held, sems):
    copies = [
        pltpu.make_async_copy(
            src.at[0, pl.ds(256 * wy, 256)], held.at[n, wy], sems.at[n, wy]
        )
        for wy in range(4)
        for n, src in enumerate((latents, cotangent))
    ]
    for copy in copies:
        copy.start()
    for wy in range(4):
        for n in range(2):
            copies[2 * wy + n].wait()
            for pair in range(4):
                rows = held[n, wy, 64 * pair : 64 * (pair + 1), :].astype(F32).reshape(2, 4, WIN, D)
                for wx in range(4):
                    both = jnp.concatenate([rows[0, wx], rows[1, wx]], axis=0).astype(BF16)
                    first = SHARE * n + 16 * pair
                    packed[4 * wy + wx, first : first + 16, :] = both


def pack(latents, cotangent):
    return pl.pallas_call(
        pack_kernel,
        in_specs=[pl.BlockSpec(memory_space=pltpu.HBM)] * 2,
        out_shape=shaped(BF16, FRAMES, 2 * SHARE, D),
        scratch_shapes=[
            pltpu.VMEM((2, 4, 256, D), BF16),
            pltpu.SemaphoreType.DMA((2, 4)),
        ],
        compiler_params=params(8),
    )(latents, cotangent)


def unpack_kernel(back, grads, qkv_t, out_t, qkv_s, out_s, gain_t, gain_s, held, sems):
    copies = []
    for wy in range(4):
        for pair in range(4):
            rows = back[4 * wy : 4 * wy + 4, 16 * pair : 16 * (pair + 1), :].astype(F32)
            for wx in range(4):
                for i in range(2):
                    start = 64 * pair + 32 * i + WIN * wx
                    held[wy, start : start + WIN, :] = rows[wx, WIN * i : WIN * (i + 1)]
        copies.append(
            pltpu.make_async_copy(held.at[wy], grads.at[0, pl.ds(256 * wy, 256)], sems.at[wy])
        )
        copies[wy].start()
    inverse = (FRAMES * TOKENS) ** (-0.5)

    def total(first, sources):
        return sum(back[f, first : first + 16, :].astype(F32) for f in sources) * inverse

    for core, qkv, out in ((0, qkv_t, out_t), (1, qkv_s, out_s)):
        sources = range(core, FRAMES, 2)
        for i in range(3):
            qkv[:, D * i : D * (i + 1)] = total(SHARE + 16 + 16 * i, sources)
        out[...] = total(SHARE + 64, sources)
    sums = total(SHARE, range(FRAMES))
    sums = sums[0:2] + sums[2:4]
    gain_t[...] = sums[0, :16]
    gain_s[...] = sums[1, :16]
    for copy in copies:
        copy.wait()


def unpack(back):
    vmem = pl.BlockSpec(memory_space=pltpu.VMEM)
    return pl.pallas_call(
        unpack_kernel,
        in_specs=[vmem],
        out_specs=[pl.BlockSpec(memory_space=pl.ANY)] + [vmem] * 6,
        out_shape=(
            shaped(F32, 1, TOKENS, D),
            shaped(F32, 16, 3 * D),
            shaped(F32, 16, D),
            shaped(F32, 16, 3 * D),
            shaped(F32, 16, D),
            shaped(F32, 16),
            shaped(F32, 16),
        ),
        scratch_shapes=[pltpu.VMEM((4, 256, D), F32), pltpu.SemaphoreType.DMA((4,))],
        compiler_params=params(8),
    )(back)


def exchange(x):
    return lax.all_to_all(x, "frame", split_axis=0, concat_axis=0, tiled=True)


def per_device(latents, cotangent, gain_time, qkv_time, out_time, gain_space, qkv_space, out_space):
    gain_time, gain_space = gain_time.reshape(1, D), gain_space.reshape(1, D)
    moved = exchange(pack(latents, cotangent))
    *state, kept, given = run_main(
        moved, gain_time, qkv_time, out_time, gain_space, qkv_space, out_space
    )
    taken = lax.ppermute(given, "frame", [(i, i ^ 1) for i in range(FRAMES)])
    grads = run_input(*state, gain_time, qkv_time)
    return tuple(unpack(exchange(join(grads, kept, taken))))


def solution(mesh):
    whole = P(("dp", "frame"), None, None)
    rows = P(("dp", "frame"), None)
    flat = P(("dp", "frame"))
    return jax.shard_map(
        per_device,
        mesh=mesh,
        in_specs=(whole, whole, P(), P(), P(), P(), P(), P()),
        out_specs=(whole, rows, rows, rows, rows, flat, flat),
        check_vma=False,
    )
```

```python
import jax
import jax.numpy as jnp
from jax import lax
from jax.experimental import pallas as pl
from jax.experimental.pallas import tpu as pltpu
from jax.sharding import PartitionSpec as P

HEADS = 8
HEAD_DIM = 32
D = 256
WIN = 8
HH = 32
WW = 32
FRAMES = 16
TOKENS = 1024
ROWS = 1024
SHARE = 64
GROUP = 128
HALF = 128
PACK = 4
CHUNK = 512
SPACE_STEP = 16
TIME_STEP = 8
EPSILON = 1e-06
SCALE = HEAD_DIM ** (-0.5)
F32 = jnp.float32
BF16 = jnp.bfloat16


def dot_nn(a, b):
    return lax.dot_general(a, b, (((1,), (0,)), ((), ())), preferred_element_type=F32)


def dot_nt(a, b):
    return lax.dot_general(a, b, (((1,), (1,)), ((), ())), preferred_element_type=F32)


def dot_tn(a, b):
    return lax.dot_general(a, b, (((0,), (0,)), ((), ())), preferred_element_type=F32)


def head_masks():
    lane = lax.broadcasted_iota(jnp.int32, (1, D), 1) // HEAD_DIM % PACK
    return [(lane == h).astype(F32).astype(BF16) for h in range(PACK)]


def spread(x, masks):
    return jnp.concatenate([x * m for m in masks], axis=0)


def halves(x):
    zero = jnp.zeros((x.shape[0], HALF), x.dtype)
    return jnp.concatenate(
        [
            jnp.concatenate([x[:, :HALF], zero], axis=1),
            jnp.concatenate([zero, x[:, HALF:]], axis=1),
        ],
        axis=0,
    )


def join_halves(x):
    n = x.shape[0] // 2
    return jnp.concatenate([x[:n, :HALF], x[n:, HALF:]], axis=1)


def each_token(f, x):
    n = x.shape[0] // 2
    return jnp.concatenate([f(x[:n]), f(x[n:])], axis=0)


def first_token():
    return lax.broadcasted_iota(jnp.int32, (32, 128), 1) < 64


def pair_scores(a, b):
    both = dot_nt(a, b)
    return jnp.where(first_token(), both[:32], both[32:])


def pair_mix(x, b):
    zero = jnp.zeros_like(x)
    one = first_token()
    both = jnp.concatenate([jnp.where(one, x, zero), jnp.where(one, zero, x)], axis=0)
    return each_token(join_halves, dot_nn(both.astype(BF16), b))


def flip_space(x):
    parts = []
    for pair in range(2):
        turned = x[:, HALF * pair : HALF * (pair + 1)].T
        parts += [turned[:SHARE], turned[SHARE:]]
    return jnp.concatenate(parts, axis=1)


def flip_time(x):
    turned = x.T
    blocks = [turned[16 * i : 16 * (i + 1)] for i in range(8)]
    lane = lax.broadcasted_iota(jnp.int32, (16, 128), 1) // 16
    for bit in range(3):
        step = 1 << bit
        upper = (lane // step) % 2 == 1
        for i in range(8):
            if not i & step:
                a, b = blocks[i], blocks[i + step]
                blocks[i] = jnp.where(upper, pltpu.roll(b, 16 * step, 1), a)
                blocks[i + step] = jnp.where(upper, b, pltpu.roll(a, 128 - 16 * step, 1))
    return jnp.concatenate(blocks, axis=0)


def softmax_keys(scores, axis):
    scores = scores * SCALE
    ex = jnp.exp(scores - jnp.max(scores, axis=axis, keepdims=True))
    return ex * (1.0 / jnp.sum(ex, axis=axis, keepdims=True))


def score_grad(probs, dprobs, axis):
    weighted = probs * dprobs
    return weighted - probs * jnp.sum(weighted, axis=axis, keepdims=True)


def norm_factor(x):
    return lax.rsqrt(jnp.mean(x * x, -1, keepdims=True) + EPSILON)


def norm_back(dinput, normed, factor, gain):
    scaled = dinput * gain
    return factor * (scaled - normed * jnp.mean(scaled * normed, -1, keepdims=True))


def rows_of(c, size=CHUNK):
    return pl.ds(pl.multiple_of(c * size, size), size)


def save(ref, rows, x):
    for half in range(2):
        ref[half, rows, :] = x[:, HALF * half : HALF * (half + 1)]


def main_kernel(
    moved, gain_t, qkv_t, out_t, gain_s, qkv_s, out_s, xs, dproj, dmid, gain_sum_s, kept, given,
    stage, in_t, proj_t, probs_t, mixed_t, middle, in_s, proj_s, mixed_s, dmix, dmid_b, parts,
):
    masks = head_masks()

    def strided(ref, first, count, stride):
        return jnp.concatenate(
            [ref[half, pl.ds(first, count, stride=stride), :] for half in range(2)], axis=1
        )

    def widen(f, _):
        save(stage, rows_of(f, SHARE), moved[f, :SHARE, :].astype(F32))
        return _

    lax.fori_loop(0, FRAMES, widen, 0)

    def by_token(ref, c):
        return jnp.concatenate([strided(ref, c * (CHUNK // 16) + i, FRAMES, SHARE) for i in range(CHUNK // 16)], axis=0)

    def by_frame(ref, c):
        return jnp.concatenate([strided(ref, c * (CHUNK // SHARE) + i, SHARE, FRAMES) for i in range(CHUNK // SHARE)], axis=0)

    def project_time(c, _):
        x = by_token(stage, c)
        xs[rows_of(c), :] = x
        inp = (x * norm_factor(x) * gain_t[...]).astype(BF16)
        in_t[rows_of(c), :] = inp
        proj_t[rows_of(c), :] = dot_nn(inp, qkv_t[...]).astype(BF16)
        return _

    lax.fori_loop(0, ROWS // CHUNK, project_time, 0, unroll=True)

    def time_pairs(c):
        return [
            pl.ds(pl.multiple_of(c * TIME_STEP * GROUP + 32 * i, 32), 32)
            for i in range(4 * TIME_STEP)
        ]

    def load(ref, offset, rows):
        return [ref[r, offset : offset + D] for r in rows]

    def spread_pairs(xs):
        return [each_token(lambda t: spread(t, masks), x) for x in xs]

    def halves_pairs(xs):
        return [each_token(halves, x) for x in xs]

    def by_four(xs):
        return [jnp.concatenate(xs[i : i + 4], axis=0) for i in range(0, len(xs), 4)]

    def in_pairs(xs):
        return [x[32 * i : 32 * (i + 1)] for x in xs for i in range(4)]

    def time_forward(c, _):
        rows = time_pairs(c)
        q, k, v = (load(proj_t, D * i, rows) for i in range(3))
        qb = spread_pairs(q)
        scores = by_four([pair_scores(x, y) for x, y in zip(halves_pairs(k), qb)])
        probs = [softmax_keys(x.reshape(8, 16, 128), 1).reshape(GROUP, 128) for x in scores]
        turned = in_pairs([flip_time(x) for x in probs])
        vb = spread_pairs(v)
        mixed = [pair_mix(x, y) for x, y in zip(turned, vb)]
        for n in range(TIME_STEP):
            probs_t[rows_of(c * TIME_STEP + n, GROUP), :] = probs[n].astype(BF16)
        for r, x in zip(rows, mixed):
            mixed_t[r, :] = x.astype(BF16)
        return _

    lax.fori_loop(0, ROWS // GROUP // TIME_STEP, time_forward, 0)

    def make_middle(c, _):
        mid = xs[rows_of(c), :] + dot_nn(mixed_t[rows_of(c), :], out_t[...])
        save(stage, rows_of(c), mid.astype(BF16).astype(F32))
        return _

    lax.fori_loop(0, ROWS // CHUNK, make_middle, 0, unroll=True)

    def cots(c):
        return moved[pl.ds(CHUNK // SHARE * c, CHUNK // SHARE), SHARE:, :].reshape(CHUNK, D)

    def project_space(c, _):
        mid = by_frame(stage, c)
        middle[rows_of(c), :] = mid
        inp = (mid * norm_factor(mid) * gain_s[...]).astype(BF16)
        in_s[rows_of(c), :] = inp
        proj_s[rows_of(c), :] = dot_nn(inp, qkv_s[...]).astype(BF16)
        dmix[rows_of(c), :] = dot_nt(cots(c), out_s[...]).astype(BF16)
        return _

    lax.fori_loop(0, ROWS // CHUNK, project_space, 0, unroll=True)

    def space(c, _):
        rows = [rows_of(c * SPACE_STEP + i, SHARE) for i in range(SPACE_STEP)]
        q, k, v = (load(proj_s, D * i, rows) for i in range(3))
        do = load(dmix, 0, rows)

        def split(x):
            return x.reshape(2, SHARE, D)

        def turn(x):
            return jnp.concatenate([flip_space(x[:SHARE]), flip_space(x[SHARE:])], axis=0)

        qb = [spread(x, masks) for x in q]
        scores = [split(dot_nt(halves(x), y)) for x, y in zip(k, qb)]
        dob = [spread(x, masks) for x in do]
        dprobs = [split(dot_nt(halves(x), y)) for x, y in zip(v, dob)]
        probs = [softmax_keys(x, 1) for x in scores]
        probs_b = [x.astype(BF16).reshape(2 * SHARE, D) for x in probs]
        ds = [score_grad(x, y, 1).astype(BF16).reshape(2 * SHARE, D) for x, y in zip(probs, dprobs)]
        turned = [turn(x) for x in probs_b]
        ds_turned = [turn(x) for x in ds]
        dv = [join_halves(dot_nn(x, y)) for x, y in zip(probs_b, dob)]
        dk = [join_halves(dot_nn(x, y)) * SCALE for x, y in zip(ds, qb)]
        mixed = [join_halves(dot_nn(x, spread(y, masks))) for x, y in zip(turned, v)]
        dq = [join_halves(dot_nn(x, spread(y, masks))) * SCALE for x, y in zip(ds_turned, k)]
        for n, r in enumerate(rows):
            mixed_s[r, :] = mixed[n].astype(BF16)
            for i, grad in enumerate((dq, dk, dv)):
                dproj[r, D * i : D * (i + 1)] = grad[n].astype(BF16)
        return _

    lax.fori_loop(0, FRAMES // SPACE_STEP, space, 0)

    def place(kind, first, sums):
        sums = sums.astype(BF16)
        for i in range(sums.shape[1] // D):
            for d in range(FRAMES):
                parts[kind, d, first + 16 * i : first + 16 * (i + 1), :] = sums[
                    16 * d : 16 * (d + 1), D * i : D * (i + 1)
                ]

    place(1, 0, dot_tn(in_s[...], dproj[...]))
    place(1, 48, dot_tn(mixed_s[...], moved[:, SHARE:, :].reshape(ROWS, D)))

    def middle_back(c, gain_sum):
        dinput = dot_nt(dproj[rows_of(c), :], qkv_s[...])
        mid = middle[rows_of(c), :]
        factor = norm_factor(mid)
        normed = mid * factor
        save(dmid, rows_of(c), cots(c).astype(F32) + norm_back(dinput, normed, factor, gain_s[...]))
        return gain_sum + jnp.sum(dinput * normed, axis=0, keepdims=True)

    gain_sum_s[...] = lax.fori_loop(0, ROWS // CHUNK, middle_back, jnp.zeros((1, D), F32), unroll=True)

    def mixed_back(c, _):
        dm = by_token(dmid, c).astype(BF16)
        dmid_b[rows_of(c), :] = dm
        dmix[rows_of(c), :] = dot_nt(dm, out_t[...]).astype(BF16)
        return _

    lax.fori_loop(0, ROWS // CHUNK, mixed_back, 0, unroll=True)

    def time_back(c, _):
        rows = time_pairs(c)
        q, k, v = (load(proj_t, D * i, rows) for i in range(3))
        do = load(dmix, 0, rows)
        groups = [rows_of(c * TIME_STEP + n, GROUP) for n in range(TIME_STEP)]
        probs = [probs_t[g, :].astype(F32) for g in groups]
        dob = spread_pairs(do)
        dprobs = by_four([pair_scores(x, y) for x, y in zip(halves_pairs(v), dob)])
        ds = [
            score_grad(x.reshape(8, 16, 128), y.reshape(8, 16, 128), 1).reshape(GROUP, 128)
            for x, y in zip(probs, dprobs)
        ]
        turned = in_pairs([flip_time(x) for x in ds])
        dv = [pair_mix(x, y) for x, y in zip(in_pairs(probs), dob)]
        dk = [pair_mix(x, y) * SCALE for x, y in zip(in_pairs(ds), spread_pairs(q))]
        dq = [pair_mix(x, y) * SCALE for x, y in zip(turned, spread_pairs(k))]
        for n, r in enumerate(rows):
            for i, grad in enumerate((dq, dk, dv)):
                dproj[r, D * i : D * (i + 1)] = grad[n].astype(BF16)
        return _

    lax.fori_loop(0, ROWS // GROUP // TIME_STEP, time_back, 0)

    place(0, 0, dot_tn(in_t[...], dproj[...]))
    place(0, 48, dot_tn(mixed_t[...], dmid_b[...]))

    core = lax.axis_index("frame") % 2
    kept[...] = parts[core]
    given[...] = parts[1 - core]


def input_kernel(xs, dproj, dmid, gain_sum_s, gain_t, qkv_t, sent, stage):
    def input_back(c, gain_sum):
        dinput = dot_nt(dproj[rows_of(c), :], qkv_t[...])
        x = xs[rows_of(c), :]
        factor = norm_factor(x)
        normed = x * factor
        save(stage, rows_of(c), norm_back(dinput, normed, factor, gain_t[...]))
        return gain_sum + jnp.sum(dinput * normed, axis=0, keepdims=True)

    gain_sum_t = lax.fori_loop(0, ROWS // CHUNK, input_back, jnp.zeros((1, D), F32), unroll=True)

    gains = jnp.concatenate([gain_sum_t, gain_sum_s[...]], axis=0)
    high = gains.astype(BF16).astype(F32)
    low = gains - high
    extra = jnp.concatenate([high, low, jnp.zeros((12, D), F32)], axis=0)
    for f in range(FRAMES):
        turned = extra if f == 0 else pltpu.roll(extra, D - 16 * f, 1)
        sent[f, SHARE:, :] = turned.astype(BF16)
        for half in range(2):
            dnorm = stage[half, pl.ds(f, SHARE, stride=FRAMES), :]
            total = dmid[half, SHARE * f : SHARE * (f + 1), :] + dnorm
            sent[f, :SHARE, HALF * half : HALF * (half + 1)] = total.astype(BF16)


def join_kernel(grads, kept, taken, sent):
    sent[:, : SHARE + 16, :] = grads[...]
    sent[:, SHARE + 16 :, :] = (kept[...].astype(F32) + taken[...].astype(F32)).astype(BF16)


def shaped(kind, *shape):
    return jax.ShapeDtypeStruct(shape, kind)


def params(mebibytes):
    return pltpu.CompilerParams(vmem_limit_bytes=mebibytes * 1024 * 1024)


def run_main(moved, gain_t, qkv_t, out_t, gain_s, qkv_s, out_s):
    def rows(width, kind):
        return pltpu.VMEM((ROWS, width), kind)

    return pl.pallas_call(
        main_kernel,
        out_shape=(
            shaped(F32, ROWS, D),
            shaped(BF16, ROWS, 3 * D),
            shaped(F32, 2, ROWS, HALF),
            shaped(F32, 1, D),
            shaped(BF16, FRAMES, SHARE, D),
            shaped(BF16, FRAMES, SHARE, D),
        ),
        scratch_shapes=[
            pltpu.VMEM((2, ROWS, HALF), F32),
            rows(D, BF16),
            rows(3 * D, BF16),
            rows(128, BF16),
            rows(D, BF16),
            rows(D, F32),
            rows(D, BF16),
            rows(3 * D, BF16),
            rows(D, BF16),
            rows(D, BF16),
            rows(D, BF16),
            pltpu.VMEM((2, FRAMES, SHARE, D), BF16),
        ],
        compiler_params=params(40),
        cost_estimate=pl.CostEstimate(
            flops=8 * 10**9, bytes_accessed=6 * 10**6, transcendentals=2 * 10**6
        ),
    )(moved, gain_t, qkv_t, out_t, gain_s, qkv_s, out_s)


def run_input(xs, dproj, dmid, gain_sum_s, gain_t, qkv_t):
    return pl.pallas_call(
        input_kernel,
        out_shape=shaped(BF16, FRAMES, SHARE + 16, D),
        scratch_shapes=[pltpu.VMEM((2, ROWS, HALF), F32)],
        compiler_params=params(16),
        cost_estimate=pl.CostEstimate(flops=2 * 10**9, bytes_accessed=6 * 10**6, transcendentals=0),
    )(xs, dproj, dmid, gain_sum_s, gain_t, qkv_t)


def join(grads, kept, taken):
    return pl.pallas_call(
        join_kernel,
        out_shape=shaped(BF16, FRAMES, 2 * SHARE + 16, D),
        compiler_params=params(8),
    )(grads, kept, taken)


def pack_kernel(latents, cotangent, packed, held, ready, sems, out_sems):
    copies = [
        [
            pltpu.make_async_copy(src.at[0, pl.ds(256 * wy, 256)], held.at[n, wy], sems.at[n, wy])
            for n, src in enumerate((latents, cotangent))
        ]
        for wy in range(4)
    ]
    for wy in range(4):
        for copy in copies[wy]:
            copy.start()
    outs = []
    for wy in range(4):
        for n in range(2):
            copies[wy][n].wait()
            for pair in range(4):
                rows = held[n, wy, 64 * pair : 64 * (pair + 1), :].astype(F32).reshape(2, 4, WIN, D)
                for wx in range(4):
                    both = jnp.concatenate([rows[0, wx], rows[1, wx]], axis=0).astype(BF16)
                    first = SHARE * n + 16 * pair
                    ready[4 * wy + wx, first : first + 16, :] = both
        outs.append(
            pltpu.make_async_copy(
                ready.at[pl.ds(4 * wy, 4)], packed.at[pl.ds(4 * wy, 4)], out_sems.at[wy]
            )
        )
        outs[wy].start()
    for copy in outs:
        copy.wait()


def pack(latents, cotangent):
    anywhere = pl.BlockSpec(memory_space=pl.ANY)
    return pl.pallas_call(
        pack_kernel,
        in_specs=[anywhere] * 2,
        out_specs=anywhere,
        out_shape=shaped(BF16, FRAMES, 2 * SHARE, D),
        scratch_shapes=[
            pltpu.VMEM((2, 4, 256, D), BF16),
            pltpu.VMEM((FRAMES, 2 * SHARE, D), BF16),
            pltpu.SemaphoreType.DMA((2, 4)),
            pltpu.SemaphoreType.DMA((4,)),
        ],
        compiler_params=params(60),
    )(latents, cotangent)


def unpack_kernel(back, grads, qkv_t, out_t, qkv_s, out_s, gain_t, gain_s, held, sems):
    copies = []
    for wy in range(4):
        for pair in range(4):
            rows = back[4 * wy : 4 * wy + 4, 16 * pair : 16 * (pair + 1), :].astype(F32)
            for wx in range(4):
                for i in range(2):
                    start = 64 * pair + 32 * i + WIN * wx
                    held[wy, start : start + WIN, :] = rows[wx, WIN * i : WIN * (i + 1)]
        copies.append(
            pltpu.make_async_copy(held.at[wy], grads.at[0, pl.ds(256 * wy, 256)], sems.at[wy])
        )
        copies[wy].start()
    inverse = (FRAMES * TOKENS) ** (-0.5)

    def total(first, sources):
        return sum(back[f, first : first + 16, :].astype(F32) for f in sources) * inverse

    for core, qkv, out in ((0, qkv_t, out_t), (1, qkv_s, out_s)):
        sources = range(core, FRAMES, 2)
        for i in range(3):
            qkv[:, D * i : D * (i + 1)] = total(SHARE + 16 + 16 * i, sources)
        out[...] = total(SHARE + 64, sources)
    sums = total(SHARE, range(FRAMES))
    sums = sums[0:2] + sums[2:4]
    gain_t[...] = sums[0, :16]
    gain_s[...] = sums[1, :16]
    for copy in copies:
        copy.wait()


def unpack(back):
    vmem = pl.BlockSpec(memory_space=pltpu.VMEM)
    return pl.pallas_call(
        unpack_kernel,
        in_specs=[vmem],
        out_specs=[pl.BlockSpec(memory_space=pl.ANY)] + [vmem] * 6,
        out_shape=(
            shaped(F32, 1, TOKENS, D),
            shaped(F32, 16, 3 * D),
            shaped(F32, 16, D),
            shaped(F32, 16, 3 * D),
            shaped(F32, 16, D),
            shaped(F32, 16),
            shaped(F32, 16),
        ),
        scratch_shapes=[pltpu.VMEM((4, 256, D), F32), pltpu.SemaphoreType.DMA((4,))],
        compiler_params=params(8),
    )(back)


def exchange(x):
    return lax.all_to_all(x, "frame", split_axis=0, concat_axis=0, tiled=True)


def per_device(latents, cotangent, gain_time, qkv_time, out_time, gain_space, qkv_space, out_space):
    gain_time, gain_space = gain_time.reshape(1, D), gain_space.reshape(1, D)
    moved = exchange(pack(latents, cotangent))
    *state, kept, given = run_main(
        moved, gain_time, qkv_time, out_time, gain_space, qkv_space, out_space
    )
    taken = lax.ppermute(given, "frame", [(i, i ^ 1) for i in range(FRAMES)])
    grads = run_input(*state, gain_time, qkv_time)
    return tuple(unpack(exchange(join(grads, kept, taken))))


def solution(mesh):
    whole = P(("dp", "frame"), None, None)
    rows = P(("dp", "frame"), None)
    flat = P(("dp", "frame"))
    return jax.shard_map(
        per_device,
        mesh=mesh,
        in_specs=(whole, whole, P(), P(), P(), P(), P(), P()),
        out_specs=(whole, rows, rows, rows, rows, flat, flat),
        check_vma=False,
    )
```

```python
import jax
import jax.numpy as jnp
from jax import lax
from jax.experimental import pallas as pl
from jax.experimental.pallas import tpu as pltpu
from jax.sharding import PartitionSpec as P

HEADS = 8
HEAD_DIM = 32
D = 256
WIN = 8
HH = 32
WW = 32
FRAMES = 16
TOKENS = 1024
ROWS = 1024
SHARE = 64
GROUP = 128
HALF = 128
PACK = 4
CHUNK = 256
SPACE_STEP = 16
TIME_STEP = 8
EPSILON = 1e-06
SCALE = HEAD_DIM ** (-0.5)
LOG2E = 1.4426950408889634
F32 = jnp.float32
BF16 = jnp.bfloat16


def dot_nn(a, b):
    return lax.dot_general(a, b, (((1,), (0,)), ((), ())), preferred_element_type=F32)


def dot_nt(a, b):
    return lax.dot_general(a, b, (((1,), (1,)), ((), ())), preferred_element_type=F32)


def dot_tn(a, b):
    return lax.dot_general(a, b, (((0,), (0,)), ((), ())), preferred_element_type=F32)


def head_masks():
    lane = lax.broadcasted_iota(jnp.int32, (1, D), 1) // HEAD_DIM % PACK
    return [(lane == h).astype(F32).astype(BF16) for h in range(PACK)]


def spread(x, masks):
    return jnp.concatenate([x * m for m in masks], axis=0)


def halves(x):
    zero = jnp.zeros((x.shape[0], HALF), x.dtype)
    return jnp.concatenate(
        [
            jnp.concatenate([x[:, :HALF], zero], axis=1),
            jnp.concatenate([zero, x[:, HALF:]], axis=1),
        ],
        axis=0,
    )


def join_halves(x):
    n = x.shape[0] // 2
    return jnp.concatenate([x[:n, :HALF], x[n:, HALF:]], axis=1)


def each_token(f, x):
    n = x.shape[0] // 2
    return jnp.concatenate([f(x[:n]), f(x[n:])], axis=0)


def first_token():
    return lax.broadcasted_iota(jnp.int32, (32, 128), 1) < 64


def pair_scores(a, b):
    both = dot_nt(a, b)
    return jnp.where(first_token(), both[:32], both[32:])


def pair_mix(x, b):
    zero = jnp.zeros_like(x)
    one = first_token()
    both = jnp.concatenate([jnp.where(one, x, zero), jnp.where(one, zero, x)], axis=0)
    return each_token(join_halves, dot_nn(both.astype(BF16), b))


def flip_space(x):
    parts = []
    for pair in range(2):
        turned = x[:, HALF * pair : HALF * (pair + 1)].T
        parts += [turned[:SHARE], turned[SHARE:]]
    return jnp.concatenate(parts, axis=1)


def flip_time(x):
    turned = x.T
    blocks = [turned[16 * i : 16 * (i + 1)] for i in range(8)]
    lane = lax.broadcasted_iota(jnp.int32, (16, 128), 1) // 16
    for bit in range(3):
        step = 1 << bit
        upper = (lane // step) % 2 == 1
        for i in range(8):
            if not i & step:
                a, b = blocks[i], blocks[i + step]
                blocks[i] = jnp.where(upper, pltpu.roll(b, 16 * step, 1), a)
                blocks[i + step] = jnp.where(upper, b, pltpu.roll(a, 128 - 16 * step, 1))
    return jnp.concatenate(blocks, axis=0)


def softmax_keys(scores, axis):
    ex = jnp.exp2((scores - jnp.max(scores, axis=axis, keepdims=True)) * (SCALE * LOG2E))
    return ex * (1.0 / jnp.sum(ex, axis=axis, keepdims=True))


def score_grad(probs, dprobs, axis):
    weighted = probs * dprobs
    return weighted - probs * jnp.sum(weighted, axis=axis, keepdims=True)


def norm_factor(x):
    return lax.rsqrt(jnp.mean(x * x, -1, keepdims=True) + EPSILON)


def norm_back(dinput, normed, factor, gain):
    scaled = dinput * gain
    return factor * (scaled - normed * jnp.mean(scaled * normed, -1, keepdims=True))


def rows_of(c, size=CHUNK):
    return pl.ds(pl.multiple_of(c * size, size), size)


def swap_matrix():
    row = lax.broadcasted_iota(jnp.int32, (CHUNK, CHUNK), 0)
    col = lax.broadcasted_iota(jnp.int32, (CHUNK, CHUNK), 1)
    return (row == col % 16 * 16 + col // 16).astype(F32).astype(BF16)


def block(ref, c, base=0):
    rows = pl.ds(base + 16 * c, 16)
    return ref[:, rows, :].reshape(CHUNK, ref.shape[2])


def put_block(ref, c, x):
    ref[:, pl.ds(16 * c, 16), :] = x.reshape(FRAMES, 16, x.shape[1])


def main_kernel(
    moved, gain_t, qkv_t, out_t, gain_s, qkv_s, out_s, xs, dproj, dmid, gain_sum_s, kept, given,
    in_t, proj_t, probs_t, mixed_t, middle, in_s, proj_s, mixed_s, dmix_s, dmix_t, dproj_s, dmid_b, parts,
):
    masks = head_masks()

    def strided(ref, first, count, stride):
        return jnp.concatenate(
            [ref[half, pl.ds(first, count, stride=stride), :] for half in range(2)], axis=1
        )

    swap = swap_matrix()

    chunks = range(ROWS // CHUNK)
    x = [dot_nn(swap, block(moved, c)) for c in chunks]
    inp = [(y * norm_factor(y) * gain_t[...]).astype(BF16) for y in x]
    proj = [dot_nn(y, qkv_t[...]).astype(BF16) for y in inp]
    for c in chunks:
        xs[rows_of(c), :] = x[c].astype(BF16)
        in_t[rows_of(c), :] = inp[c]
        proj_t[rows_of(c), :] = proj[c]

    def time_pairs(c):
        return [
            pl.ds(pl.multiple_of(c * TIME_STEP * GROUP + 32 * i, 32), 32)
            for i in range(4 * TIME_STEP)
        ]

    def load(ref, offset, rows):
        return [ref[r, offset : offset + D] for r in rows]

    def spread_pairs(xs):
        return [each_token(lambda t: spread(t, masks), x) for x in xs]

    def halves_pairs(xs):
        return [each_token(halves, x) for x in xs]

    def by_four(xs):
        return [jnp.concatenate(xs[i : i + 4], axis=0) for i in range(0, len(xs), 4)]

    def in_pairs(xs):
        return [x[32 * i : 32 * (i + 1)] for x in xs for i in range(4)]

    def time_forward(c, _):
        rows = time_pairs(c)
        q, k, v = (load(proj_t, D * i, rows) for i in range(3))
        qb = spread_pairs(q)
        scores = by_four([pair_scores(x, y) for x, y in zip(halves_pairs(k), qb)])
        probs = [softmax_keys(x.reshape(8, 16, 128), 1).reshape(GROUP, 128) for x in scores]
        turned = in_pairs([flip_time(x) for x in probs])
        vb = spread_pairs(v)
        mixed = [pair_mix(x, y) for x, y in zip(turned, vb)]
        for n in range(TIME_STEP):
            probs_t[rows_of(c * TIME_STEP + n, GROUP), :] = probs[n].astype(BF16)
        for r, x in zip(rows, mixed):
            mixed_t[r, :] = x.astype(BF16)
        return _

    lax.fori_loop(0, ROWS // GROUP // TIME_STEP, time_forward, 0)

    dmix = [dot_nt(block(moved, c, SHARE), out_s[...]).astype(BF16) for c in chunks]
    mid = [xs[rows_of(c), :].astype(F32) + dot_nn(mixed_t[rows_of(c), :], out_t[...]) for c in chunks]
    mid = [dot_nn(swap, y.astype(BF16)) for y in mid]
    inp = [(y * norm_factor(y) * gain_s[...]).astype(BF16) for y in mid]
    proj = [dot_nn(y, qkv_s[...]).astype(BF16) for y in inp]
    for c in chunks:
        put_block(dmix_s, c, dmix[c])
        put_block(middle, c, mid[c])
        put_block(in_s, c, inp[c])
        put_block(proj_s, c, proj[c])

    def space(c, _):
        rows = [c * SPACE_STEP + i for i in range(SPACE_STEP)]
        q, k, v = ([proj_s[r, :, D * i : D * (i + 1)] for r in rows] for i in range(3))
        do = [dmix_s[r] for r in rows]

        def split(x):
            return x.reshape(2, SHARE, D)

        def turn(x):
            return jnp.concatenate([flip_space(x[:SHARE]), flip_space(x[SHARE:])], axis=0)

        qb = [spread(x, masks) for x in q]
        scores = [split(dot_nt(halves(x), y)) for x, y in zip(k, qb)]
        dob = [spread(x, masks) for x in do]
        dprobs = [split(dot_nt(halves(x), y)) for x, y in zip(v, dob)]
        probs = [softmax_keys(x, 1) for x in scores]
        probs_b = [x.astype(BF16).reshape(2 * SHARE, D) for x in probs]
        ds = [score_grad(x, y, 1).astype(BF16).reshape(2 * SHARE, D) for x, y in zip(probs, dprobs)]
        turned = [turn(x) for x in probs_b]
        ds_turned = [turn(x) for x in ds]
        dv = [join_halves(dot_nn(x, y)) for x, y in zip(probs_b, dob)]
        dk = [join_halves(dot_nn(x, y)) * SCALE for x, y in zip(ds, qb)]
        mixed = [join_halves(dot_nn(x, spread(y, masks))) for x, y in zip(turned, v)]
        dq = [join_halves(dot_nn(x, spread(y, masks))) * SCALE for x, y in zip(ds_turned, k)]
        for n, r in enumerate(rows):
            mixed_s[r] = mixed[n].astype(BF16)
            for i, grad in enumerate((dq, dk, dv)):
                dproj_s[r, :, D * i : D * (i + 1)] = grad[n].astype(BF16)
        return _

    lax.fori_loop(0, FRAMES // SPACE_STEP, space, 0)

    def place(kind, first, sums):
        sums = sums.astype(BF16)
        for i in range(sums.shape[1] // D):
            for d in range(FRAMES):
                parts[kind, d, first + 16 * i : first + 16 * (i + 1), :] = sums[
                    16 * d : 16 * (d + 1), D * i : D * (i + 1)
                ]

    def flat(ref):
        return ref[...].reshape(ROWS, ref.shape[2])

    place(1, 0, dot_tn(flat(in_s), flat(dproj_s)))
    place(1, 48, dot_tn(flat(mixed_s), moved[:, SHARE:, :].reshape(ROWS, D)))

    dinput = [dot_nt(block(dproj_s, c), qkv_s[...]) for c in chunks]
    mid = [block(middle, c) for c in chunks]
    factor = [norm_factor(y) for y in mid]
    normed = [y * f for y, f in zip(mid, factor)]
    dnorm = [norm_back(d, n, f, gain_s[...]) for d, n, f in zip(dinput, normed, factor)]
    dm = [block(moved, c, SHARE).astype(F32) + dnorm[c] for c in chunks]
    dm_b = [dot_nn(swap, y.astype(BF16)).astype(BF16) for y in dm]
    dmix = [dot_nt(y, out_t[...]).astype(BF16) for y in dm_b]
    for c in chunks:
        put_block(dmid, c, dm[c])
        dmid_b[rows_of(c), :] = dm_b[c]
        dmix_t[rows_of(c), :] = dmix[c]
    gain_sum_s[...] = sum(
        jnp.sum(d * n, axis=0, keepdims=True) for d, n in zip(dinput, normed)
    )

    def time_back(c, _):
        rows = time_pairs(c)
        q, k, v = (load(proj_t, D * i, rows) for i in range(3))
        do = load(dmix_t, 0, rows)
        groups = [rows_of(c * TIME_STEP + n, GROUP) for n in range(TIME_STEP)]
        probs = [probs_t[g, :].astype(F32) for g in groups]
        dob = spread_pairs(do)
        dprobs = by_four([pair_scores(x, y) for x, y in zip(halves_pairs(v), dob)])
        ds = [
            score_grad(x.reshape(8, 16, 128), y.reshape(8, 16, 128), 1).reshape(GROUP, 128)
            for x, y in zip(probs, dprobs)
        ]
        turned = in_pairs([flip_time(x) for x in ds])
        dv = [pair_mix(x, y) for x, y in zip(in_pairs(probs), dob)]
        dk = [pair_mix(x, y) * SCALE for x, y in zip(in_pairs(ds), spread_pairs(q))]
        dq = [pair_mix(x, y) * SCALE for x, y in zip(turned, spread_pairs(k))]
        for n, r in enumerate(rows):
            for i, grad in enumerate((dq, dk, dv)):
                dproj[r, D * i : D * (i + 1)] = grad[n].astype(BF16)
        return _

    lax.fori_loop(0, ROWS // GROUP // TIME_STEP, time_back, 0)

    place(0, 0, dot_tn(in_t[...], dproj[...]))
    place(0, 48, dot_tn(mixed_t[...], dmid_b[...]))

    core = lax.axis_index("frame") % 2
    kept[...] = parts[core]
    given[...] = parts[1 - core]


def input_kernel(xs, dproj, dmid, gain_sum_s, gain_t, qkv_t, sent):
    swap = swap_matrix()
    chunks = range(ROWS // CHUNK)
    dinput = [dot_nt(dproj[rows_of(c), :], qkv_t[...]) for c in chunks]
    x = [xs[rows_of(c), :].astype(F32) for c in chunks]
    factor = [norm_factor(y) for y in x]
    normed = [y * f for y, f in zip(x, factor)]
    dnorm = [norm_back(d, n, f, gain_t[...]) for d, n, f in zip(dinput, normed, factor)]
    dnorm = [dot_nn(swap, y.astype(BF16)) for y in dnorm]
    for c in chunks:
        put_block(sent, c, (block(dmid, c) + dnorm[c]).astype(BF16))
    gain_sum_t = sum(jnp.sum(d * n, axis=0, keepdims=True) for d, n in zip(dinput, normed))

    gains = jnp.concatenate([gain_sum_t, gain_sum_s[...]], axis=0)
    high = gains.astype(BF16).astype(F32)
    low = gains - high
    extra = jnp.concatenate([high, low, jnp.zeros((12, D), F32)], axis=0)
    for f in range(FRAMES):
        turned = extra if f == 0 else pltpu.roll(extra, D - 16 * f, 1)
        sent[f, SHARE:, :] = turned.astype(BF16)


def join_kernel(grads, kept, taken, sent):
    sent[:, : SHARE + 16, :] = grads[...]
    sent[:, SHARE + 16 :, :] = (kept[...].astype(F32) + taken[...].astype(F32)).astype(BF16)


def shaped(kind, *shape):
    return jax.ShapeDtypeStruct(shape, kind)


def params(mebibytes):
    return pltpu.CompilerParams(vmem_limit_bytes=mebibytes * 1024 * 1024)


def run_main(moved, gain_t, qkv_t, out_t, gain_s, qkv_s, out_s):
    def rows(width, kind):
        return pltpu.VMEM((ROWS, width), kind)

    def frames(width, kind):
        return pltpu.VMEM((FRAMES, SHARE, width), kind)

    return pl.pallas_call(
        main_kernel,
        out_shape=(
            shaped(BF16, ROWS, D),
            shaped(BF16, ROWS, 3 * D),
            shaped(F32, FRAMES, SHARE, D),
            shaped(F32, 1, D),
            shaped(BF16, FRAMES, SHARE, D),
            shaped(BF16, FRAMES, SHARE, D),
        ),
        scratch_shapes=[
            rows(D, BF16),
            rows(3 * D, BF16),
            rows(128, BF16),
            rows(D, BF16),
            frames(D, F32),
            frames(D, BF16),
            frames(3 * D, BF16),
            frames(D, BF16),
            frames(D, BF16),
            rows(D, BF16),
            frames(3 * D, BF16),
            rows(D, BF16),
            pltpu.VMEM((2, FRAMES, SHARE, D), BF16),
        ],
        compiler_params=params(40),
        cost_estimate=pl.CostEstimate(
            flops=8 * 10**9, bytes_accessed=6 * 10**6, transcendentals=2 * 10**6
        ),
    )(moved, gain_t, qkv_t, out_t, gain_s, qkv_s, out_s)


def run_input(xs, dproj, dmid, gain_sum_s, gain_t, qkv_t):
    return pl.pallas_call(
        input_kernel,
        out_shape=shaped(BF16, FRAMES, SHARE + 16, D),
        compiler_params=params(16),
        cost_estimate=pl.CostEstimate(flops=2 * 10**9, bytes_accessed=6 * 10**6, transcendentals=0),
    )(xs, dproj, dmid, gain_sum_s, gain_t, qkv_t)


def join(grads, kept, taken):
    return pl.pallas_call(
        join_kernel,
        out_shape=shaped(BF16, FRAMES, 2 * SHARE + 16, D),
        compiler_params=params(8),
    )(grads, kept, taken)


def pack_kernel(latents, cotangent, packed, held, ready, sems, out_sems):
    copies = [
        [
            pltpu.make_async_copy(src.at[0, pl.ds(256 * wy, 256)], held.at[n, wy], sems.at[n, wy])
            for n, src in enumerate((latents, cotangent))
        ]
        for wy in range(4)
    ]
    for wy in range(4):
        for copy in copies[wy]:
            copy.start()
    outs = []
    for wy in range(4):
        for n in range(2):
            copies[wy][n].wait()
            for pair in range(4):
                rows = held[n, wy, 64 * pair : 64 * (pair + 1), :].astype(F32).reshape(2, 4, WIN, D)
                for wx in range(4):
                    both = jnp.concatenate([rows[0, wx], rows[1, wx]], axis=0).astype(BF16)
                    first = SHARE * n + 16 * pair
                    ready[4 * wy + wx, first : first + 16, :] = both
        outs.append(
            pltpu.make_async_copy(
                ready.at[pl.ds(4 * wy, 4)], packed.at[pl.ds(4 * wy, 4)], out_sems.at[wy]
            )
        )
        outs[wy].start()
    for copy in outs:
        copy.wait()


def pack(latents, cotangent):
    anywhere = pl.BlockSpec(memory_space=pl.ANY)
    return pl.pallas_call(
        pack_kernel,
        in_specs=[anywhere] * 2,
        out_specs=anywhere,
        out_shape=shaped(BF16, FRAMES, 2 * SHARE, D),
        scratch_shapes=[
            pltpu.VMEM((2, 4, 256, D), BF16),
            pltpu.VMEM((FRAMES, 2 * SHARE, D), BF16),
            pltpu.SemaphoreType.DMA((2, 4)),
            pltpu.SemaphoreType.DMA((4,)),
        ],
        compiler_params=params(60),
    )(latents, cotangent)


def unpack_kernel(back, grads, qkv_t, out_t, qkv_s, out_s, gain_t, gain_s, held, sems):
    copies = []
    for wy in range(4):
        for pair in range(4):
            rows = back[4 * wy : 4 * wy + 4, 16 * pair : 16 * (pair + 1), :].astype(F32)
            for wx in range(4):
                for i in range(2):
                    start = 64 * pair + 32 * i + WIN * wx
                    held[wy, start : start + WIN, :] = rows[wx, WIN * i : WIN * (i + 1)]
        copies.append(
            pltpu.make_async_copy(held.at[wy], grads.at[0, pl.ds(256 * wy, 256)], sems.at[wy])
        )
        copies[wy].start()
    inverse = (FRAMES * TOKENS) ** (-0.5)

    def total(first, sources):
        return sum(back[f, first : first + 16, :].astype(F32) for f in sources) * inverse

    for core, qkv, out in ((0, qkv_t, out_t), (1, qkv_s, out_s)):
        sources = range(core, FRAMES, 2)
        for i in range(3):
            qkv[:, D * i : D * (i + 1)] = total(SHARE + 16 + 16 * i, sources)
        out[...] = total(SHARE + 64, sources)
    sums = total(SHARE, range(FRAMES))
    sums = sums[0:2] + sums[2:4]
    gain_t[...] = sums[0, :16]
    gain_s[...] = sums[1, :16]
    for copy in copies:
        copy.wait()


def unpack(back):
    vmem = pl.BlockSpec(memory_space=pltpu.VMEM)
    return pl.pallas_call(
        unpack_kernel,
        in_specs=[vmem],
        out_specs=[pl.BlockSpec(memory_space=pl.ANY)] + [vmem] * 6,
        out_shape=(
            shaped(F32, 1, TOKENS, D),
            shaped(F32, 16, 3 * D),
            shaped(F32, 16, D),
            shaped(F32, 16, 3 * D),
            shaped(F32, 16, D),
            shaped(F32, 16),
            shaped(F32, 16),
        ),
        scratch_shapes=[pltpu.VMEM((4, 256, D), F32), pltpu.SemaphoreType.DMA((4,))],
        compiler_params=params(8),
    )(back)


def exchange(x):
    return lax.all_to_all(x, "frame", split_axis=0, concat_axis=0, tiled=True)


def per_device(latents, cotangent, gain_time, qkv_time, out_time, gain_space, qkv_space, out_space):
    gain_time, gain_space = gain_time.reshape(1, D), gain_space.reshape(1, D)
    moved = exchange(pack(latents, cotangent))
    *state, kept, given = run_main(
        moved, gain_time, qkv_time, out_time, gain_space, qkv_space, out_space
    )
    taken = lax.ppermute(given, "frame", [(i, i ^ 1) for i in range(FRAMES)])
    grads = run_input(*state, gain_time, qkv_time)
    return tuple(unpack(exchange(join(grads, kept, taken))))


def solution(mesh):
    whole = P(("dp", "frame"), None, None)
    rows = P(("dp", "frame"), None)
    flat = P(("dp", "frame"))
    return jax.shard_map(
        per_device,
        mesh=mesh,
        in_specs=(whole, whole, P(), P(), P(), P(), P(), P()),
        out_specs=(whole, rows, rows, rows, rows, flat, flat),
        check_vma=False,
    )
```

```python
import jax
import jax.numpy as jnp
from jax import lax
from jax.experimental import pallas as pl
from jax.experimental.pallas import tpu as pltpu
from jax.sharding import PartitionSpec as P

HEADS = 8
HEAD_DIM = 32
D = 256
WIN = 8
HH = 32
WW = 32
FRAMES = 16
TOKENS = 1024
ROWS = 1024
SHARE = 64
GROUP = 128
HALF = 128
PACK = 4
CHUNK = 256
SPACE_STEP = 16
TIME_STEP = 8
EPSILON = 1e-06
SCALE = HEAD_DIM ** (-0.5)
LOG2E = 1.4426950408889634
F32 = jnp.float32
BF16 = jnp.bfloat16


def dot_nn(a, b):
    return lax.dot_general(a, b, (((1,), (0,)), ((), ())), preferred_element_type=F32)


def dot_nt(a, b):
    return lax.dot_general(a, b, (((1,), (1,)), ((), ())), preferred_element_type=F32)


def dot_tn(a, b):
    return lax.dot_general(a, b, (((0,), (0,)), ((), ())), preferred_element_type=F32)


def head_masks():
    lane = lax.broadcasted_iota(jnp.int32, (1, D), 1) // HEAD_DIM % PACK
    return [(lane == h).astype(F32).astype(BF16) for h in range(PACK)]


def spread(x, masks):
    return jnp.concatenate([x * m for m in masks], axis=0)


def halves(x):
    zero = jnp.zeros((x.shape[0], HALF), x.dtype)
    return jnp.concatenate(
        [
            jnp.concatenate([x[:, :HALF], zero], axis=1),
            jnp.concatenate([zero, x[:, HALF:]], axis=1),
        ],
        axis=0,
    )


def join_halves(x):
    n = x.shape[0] // 2
    return jnp.concatenate([x[:n, :HALF], x[n:, HALF:]], axis=1)


def each_token(f, x):
    n = x.shape[0] // 2
    return jnp.concatenate([f(x[:n]), f(x[n:])], axis=0)


def first_token():
    return lax.broadcasted_iota(jnp.int32, (32, 128), 1) < 64


def pair_scores(a, b):
    both = dot_nt(a, b)
    return jnp.where(first_token(), both[:32], both[32:])


def pair_mix(x, b):
    zero = jnp.zeros_like(x)
    one = first_token()
    both = jnp.concatenate([jnp.where(one, x, zero), jnp.where(one, zero, x)], axis=0)
    return each_token(join_halves, dot_nn(both.astype(BF16), b))


def flip_space(x):
    parts = []
    for pair in range(2):
        turned = x[:, HALF * pair : HALF * (pair + 1)].T
        parts += [turned[:SHARE], turned[SHARE:]]
    return jnp.concatenate(parts, axis=1)


def flip_time(x):
    turned = x.T
    blocks = [turned[16 * i : 16 * (i + 1)] for i in range(8)]
    lane = lax.broadcasted_iota(jnp.int32, (16, 128), 1) // 16
    for bit in range(3):
        step = 1 << bit
        upper = (lane // step) % 2 == 1
        for i in range(8):
            if not i & step:
                a, b = blocks[i], blocks[i + step]
                blocks[i] = jnp.where(upper, pltpu.roll(b, 16 * step, 1), a)
                blocks[i + step] = jnp.where(upper, b, pltpu.roll(a, 128 - 16 * step, 1))
    return jnp.concatenate(blocks, axis=0)


def softmax_keys(scores, axis):
    ex = jnp.exp2((scores - jnp.max(scores, axis=axis, keepdims=True)) * (SCALE * LOG2E))
    return ex * (1.0 / jnp.sum(ex, axis=axis, keepdims=True))


def score_grad(probs, dprobs, axis):
    weighted = probs * dprobs
    return weighted - probs * jnp.sum(weighted, axis=axis, keepdims=True)


def norm_factor(x):
    return lax.rsqrt(jnp.mean(x * x, -1, keepdims=True) + EPSILON)


def norm_back(dinput, normed, factor, gain):
    scaled = dinput * gain
    return factor * (scaled - normed * jnp.mean(scaled * normed, -1, keepdims=True))


def rows_of(c, size=CHUNK):
    return pl.ds(pl.multiple_of(c * size, size), size)


def swap_matrix():
    row = lax.broadcasted_iota(jnp.int32, (CHUNK, CHUNK), 0)
    col = lax.broadcasted_iota(jnp.int32, (CHUNK, CHUNK), 1)
    return (row == col % 16 * 16 + col // 16).astype(F32).astype(BF16)


def block(ref, c, base=0):
    rows = pl.ds(base + 16 * c, 16)
    return ref[:, rows, :].reshape(CHUNK, ref.shape[2])


def put_block(ref, c, x):
    ref[:, pl.ds(16 * c, 16), :] = x.reshape(FRAMES, 16, x.shape[1])


def main_kernel(
    moved, gain_t, qkv_t, out_t, gain_s, qkv_s, out_s, xs, dproj, dmid, kept, given,
    in_t, proj_t, probs_t, mixed_t, middle, in_s, proj_s, mixed_s, dmix_s, dmix_t, dproj_s, dmid_b, parts,
):
    masks = head_masks()

    def strided(ref, first, count, stride):
        return jnp.concatenate(
            [ref[half, pl.ds(first, count, stride=stride), :] for half in range(2)], axis=1
        )

    swap = swap_matrix()

    chunks = range(ROWS // CHUNK)
    x = [dot_nn(swap, block(moved, c)) for c in chunks]
    inp = [(y * norm_factor(y) * gain_t[...]).astype(BF16) for y in x]
    proj = [dot_nn(y, qkv_t[...]).astype(BF16) for y in inp]
    for c in chunks:
        xs[rows_of(c), :] = x[c].astype(BF16)
        in_t[rows_of(c), :] = inp[c]
        proj_t[rows_of(c), :] = proj[c]

    def time_pairs(c):
        return [
            pl.ds(pl.multiple_of(c * TIME_STEP * GROUP + 32 * i, 32), 32)
            for i in range(4 * TIME_STEP)
        ]

    def load(ref, offset, rows):
        return [ref[r, offset : offset + D] for r in rows]

    def spread_pairs(xs):
        return [each_token(lambda t: spread(t, masks), x) for x in xs]

    def halves_pairs(xs):
        return [each_token(halves, x) for x in xs]

    def by_four(xs):
        return [jnp.concatenate(xs[i : i + 4], axis=0) for i in range(0, len(xs), 4)]

    def in_pairs(xs):
        return [x[32 * i : 32 * (i + 1)] for x in xs for i in range(4)]

    def time_forward(c, _):
        rows = time_pairs(c)
        q, k, v = (load(proj_t, D * i, rows) for i in range(3))
        qb = spread_pairs(q)
        scores = by_four([pair_scores(x, y) for x, y in zip(halves_pairs(k), qb)])
        probs = [softmax_keys(x.reshape(8, 16, 128), 1).reshape(GROUP, 128) for x in scores]
        turned = in_pairs([flip_time(x) for x in probs])
        vb = spread_pairs(v)
        mixed = [pair_mix(x, y) for x, y in zip(turned, vb)]
        for n in range(TIME_STEP):
            probs_t[rows_of(c * TIME_STEP + n, GROUP), :] = probs[n].astype(BF16)
        for r, x in zip(rows, mixed):
            mixed_t[r, :] = x.astype(BF16)
        return _

    lax.fori_loop(0, ROWS // GROUP // TIME_STEP, time_forward, 0)

    dmix = [dot_nt(block(moved, c, SHARE), out_s[...]).astype(BF16) for c in chunks]
    mid = [xs[rows_of(c), :].astype(F32) + dot_nn(mixed_t[rows_of(c), :], out_t[...]) for c in chunks]
    mid = [dot_nn(swap, y.astype(BF16)) for y in mid]
    inp = [(y * norm_factor(y) * gain_s[...]).astype(BF16) for y in mid]
    proj = [dot_nn(y, qkv_s[...]).astype(BF16) for y in inp]
    for c in chunks:
        put_block(dmix_s, c, dmix[c])
        put_block(middle, c, mid[c])
        put_block(in_s, c, inp[c])
        put_block(proj_s, c, proj[c])

    def space(c, _):
        rows = [c * SPACE_STEP + i for i in range(SPACE_STEP)]
        q, k, v = ([proj_s[r, :, D * i : D * (i + 1)] for r in rows] for i in range(3))
        do = [dmix_s[r] for r in rows]

        def split(x):
            return x.reshape(2, SHARE, D)

        def turn(x):
            return jnp.concatenate([flip_space(x[:SHARE]), flip_space(x[SHARE:])], axis=0)

        qb = [spread(x, masks) for x in q]
        scores = [split(dot_nt(halves(x), y)) for x, y in zip(k, qb)]
        dob = [spread(x, masks) for x in do]
        dprobs = [split(dot_nt(halves(x), y)) for x, y in zip(v, dob)]
        probs = [softmax_keys(x, 1) for x in scores]
        probs_b = [x.astype(BF16).reshape(2 * SHARE, D) for x in probs]
        ds = [score_grad(x, y, 1).astype(BF16).reshape(2 * SHARE, D) for x, y in zip(probs, dprobs)]
        turned = [turn(x) for x in probs_b]
        ds_turned = [turn(x) for x in ds]
        dv = [join_halves(dot_nn(x, y)) for x, y in zip(probs_b, dob)]
        dk = [join_halves(dot_nn(x, y)) * SCALE for x, y in zip(ds, qb)]
        mixed = [join_halves(dot_nn(x, spread(y, masks))) for x, y in zip(turned, v)]
        dq = [join_halves(dot_nn(x, spread(y, masks))) * SCALE for x, y in zip(ds_turned, k)]
        for n, r in enumerate(rows):
            mixed_s[r] = mixed[n].astype(BF16)
            for i, grad in enumerate((dq, dk, dv)):
                dproj_s[r, :, D * i : D * (i + 1)] = grad[n].astype(BF16)
        return _

    lax.fori_loop(0, FRAMES // SPACE_STEP, space, 0)

    def place(kind, first, sums):
        sums = sums.astype(BF16)
        for i in range(sums.shape[1] // D):
            for d in range(FRAMES):
                parts[kind, d, first + 16 * i : first + 16 * (i + 1), :] = sums[
                    16 * d : 16 * (d + 1), D * i : D * (i + 1)
                ]

    def flat(ref):
        return ref[...].reshape(ROWS, ref.shape[2])

    place(1, 0, dot_tn(flat(in_s), flat(dproj_s)))
    place(1, 48, dot_tn(flat(mixed_s), moved[:, SHARE:, :].reshape(ROWS, D)))

    dinput = [dot_nt(block(dproj_s, c), qkv_s[...]) for c in chunks]
    mid = [block(middle, c) for c in chunks]
    factor = [norm_factor(y) for y in mid]
    normed = [y * f for y, f in zip(mid, factor)]
    dnorm = [norm_back(d, n, f, gain_s[...]) for d, n, f in zip(dinput, normed, factor)]
    dm = [block(moved, c, SHARE).astype(F32) + dnorm[c] for c in chunks]
    dm_b = [dot_nn(swap, y.astype(BF16)).astype(BF16) for y in dm]
    dmix = [dot_nt(y, out_t[...]).astype(BF16) for y in dm_b]
    for c in chunks:
        put_block(dmid, c, dm[c])
        dmid_b[rows_of(c), :] = dm_b[c]
        dmix_t[rows_of(c), :] = dmix[c]

    def time_back(c, _):
        rows = time_pairs(c)
        q, k, v = (load(proj_t, D * i, rows) for i in range(3))
        do = load(dmix_t, 0, rows)
        groups = [rows_of(c * TIME_STEP + n, GROUP) for n in range(TIME_STEP)]
        probs = [probs_t[g, :].astype(F32) for g in groups]
        dob = spread_pairs(do)
        dprobs = by_four([pair_scores(x, y) for x, y in zip(halves_pairs(v), dob)])
        ds = [
            score_grad(x.reshape(8, 16, 128), y.reshape(8, 16, 128), 1).reshape(GROUP, 128)
            for x, y in zip(probs, dprobs)
        ]
        turned = in_pairs([flip_time(x) for x in ds])
        dv = [pair_mix(x, y) for x, y in zip(in_pairs(probs), dob)]
        dk = [pair_mix(x, y) * SCALE for x, y in zip(in_pairs(ds), spread_pairs(q))]
        dq = [pair_mix(x, y) * SCALE for x, y in zip(turned, spread_pairs(k))]
        for n, r in enumerate(rows):
            for i, grad in enumerate((dq, dk, dv)):
                dproj[r, D * i : D * (i + 1)] = grad[n].astype(BF16)
        return _

    lax.fori_loop(0, ROWS // GROUP // TIME_STEP, time_back, 0)

    place(0, 0, dot_tn(in_t[...], dproj[...]))
    place(0, 48, dot_tn(mixed_t[...], dmid_b[...]))

    core = lax.axis_index("frame") % 2
    kept[...] = parts[core]
    given[...] = parts[1 - core]


def input_kernel(xs, dproj, dmid, gain_t, qkv_t, sent):
    swap = swap_matrix()
    chunks = range(ROWS // CHUNK)
    dinput = [dot_nt(dproj[rows_of(c), :], qkv_t[...]) for c in chunks]
    x = [xs[rows_of(c), :].astype(F32) for c in chunks]
    factor = [norm_factor(y) for y in x]
    normed = [y * f for y, f in zip(x, factor)]
    dnorm = [norm_back(d, n, f, gain_t[...]) for d, n, f in zip(dinput, normed, factor)]
    dnorm = [dot_nn(swap, y.astype(BF16)) for y in dnorm]
    for c in chunks:
        put_block(sent, c, (block(dmid, c) + dnorm[c]).astype(BF16))


def join_kernel(grads, kept, taken, sent):
    sent[:, :SHARE, :] = grads[...]
    sent[:, SHARE:, :] = (kept[...].astype(F32) + taken[...].astype(F32)).astype(BF16)


def shaped(kind, *shape):
    return jax.ShapeDtypeStruct(shape, kind)


def params(mebibytes):
    return pltpu.CompilerParams(vmem_limit_bytes=mebibytes * 1024 * 1024)


def run_main(moved, gain_t, qkv_t, out_t, gain_s, qkv_s, out_s):
    def rows(width, kind):
        return pltpu.VMEM((ROWS, width), kind)

    def frames(width, kind):
        return pltpu.VMEM((FRAMES, SHARE, width), kind)

    return pl.pallas_call(
        main_kernel,
        out_shape=(
            shaped(BF16, ROWS, D),
            shaped(BF16, ROWS, 3 * D),
            shaped(F32, FRAMES, SHARE, D),
            shaped(BF16, FRAMES, SHARE, D),
            shaped(BF16, FRAMES, SHARE, D),
        ),
        scratch_shapes=[
            rows(D, BF16),
            rows(3 * D, BF16),
            rows(128, BF16),
            rows(D, BF16),
            frames(D, F32),
            frames(D, BF16),
            frames(3 * D, BF16),
            frames(D, BF16),
            frames(D, BF16),
            rows(D, BF16),
            frames(3 * D, BF16),
            rows(D, BF16),
            pltpu.VMEM((2, FRAMES, SHARE, D), BF16),
        ],
        compiler_params=params(40),
        cost_estimate=pl.CostEstimate(
            flops=8 * 10**9, bytes_accessed=6 * 10**6, transcendentals=2 * 10**6
        ),
    )(moved, gain_t, qkv_t, out_t, gain_s, qkv_s, out_s)


def run_input(xs, dproj, dmid, gain_t, qkv_t):
    return pl.pallas_call(
        input_kernel,
        out_shape=shaped(BF16, FRAMES, SHARE, D),
        compiler_params=params(16),
        cost_estimate=pl.CostEstimate(flops=2 * 10**9, bytes_accessed=6 * 10**6, transcendentals=0),
    )(xs, dproj, dmid, gain_t, qkv_t)


def join(grads, kept, taken):
    return pl.pallas_call(
        join_kernel,
        out_shape=shaped(BF16, FRAMES, 2 * SHARE, D),
        compiler_params=params(8),
    )(grads, kept, taken)


def pack_kernel(latents, cotangent, packed, held, ready, sems, out_sems):
    copies = [
        [
            pltpu.make_async_copy(src.at[0, pl.ds(256 * wy, 256)], held.at[n, wy], sems.at[n, wy])
            for n, src in enumerate((latents, cotangent))
        ]
        for wy in range(4)
    ]
    for wy in range(4):
        for copy in copies[wy]:
            copy.start()
    outs = []
    for wy in range(4):
        for n in range(2):
            copies[wy][n].wait()
            for pair in range(4):
                rows = held[n, wy, 64 * pair : 64 * (pair + 1), :].astype(F32).reshape(2, 4, WIN, D)
                for wx in range(4):
                    both = jnp.concatenate([rows[0, wx], rows[1, wx]], axis=0).astype(BF16)
                    first = SHARE * n + 16 * pair
                    ready[4 * wy + wx, first : first + 16, :] = both
        outs.append(
            pltpu.make_async_copy(
                ready.at[pl.ds(4 * wy, 4)], packed.at[pl.ds(4 * wy, 4)], out_sems.at[wy]
            )
        )
        outs[wy].start()
    for copy in outs:
        copy.wait()


def pack(latents, cotangent):
    anywhere = pl.BlockSpec(memory_space=pl.ANY)
    return pl.pallas_call(
        pack_kernel,
        in_specs=[anywhere] * 2,
        out_specs=anywhere,
        out_shape=shaped(BF16, FRAMES, 2 * SHARE, D),
        scratch_shapes=[
            pltpu.VMEM((2, 4, 256, D), BF16),
            pltpu.VMEM((FRAMES, 2 * SHARE, D), BF16),
            pltpu.SemaphoreType.DMA((2, 4)),
            pltpu.SemaphoreType.DMA((4,)),
        ],
        compiler_params=params(60),
    )(latents, cotangent)


def gain_sums(sums, weights, gain, me):
    own = weights[pl.ds(pl.multiple_of(16 * me, 16), 16), :].astype(F32)
    column = jnp.sum(own * sums, axis=-1, keepdims=True)
    row = jnp.broadcast_to(column, (16, 128)).T[:1, :]
    turned = pltpu.roll(jnp.broadcast_to(gain[...], (8, D)), (D - 16 * me) % D, 1)
    return row / turned[:1, :16]


def unpack_kernel(
    back, gains_t, weights_t, gains_s, weights_s,
    grads, qkv_t, out_t, qkv_s, out_s, gain_t, gain_s, held, sems,
):
    copies = []
    for wy in range(4):
        for pair in range(4):
            rows = back[4 * wy : 4 * wy + 4, 16 * pair : 16 * (pair + 1), :].astype(F32)
            for wx in range(4):
                for i in range(2):
                    start = 64 * pair + 32 * i + WIN * wx
                    held[wy, start : start + WIN, :] = rows[wx, WIN * i : WIN * (i + 1)]
        copies.append(
            pltpu.make_async_copy(held.at[wy], grads.at[0, pl.ds(256 * wy, 256)], sems.at[wy])
        )
        copies[wy].start()
    inverse = (FRAMES * TOKENS) ** (-0.5)

    def total(first, sources):
        return sum(back[f, first : first + 16, :].astype(F32) for f in sources) * inverse

    me = lax.axis_index("frame")
    for core, qkv, out, gain, weights, gain_out in (
        (0, qkv_t, out_t, gains_t, weights_t, gain_t),
        (1, qkv_s, out_s, gains_s, weights_s, gain_s),
    ):
        sources = range(core, FRAMES, 2)
        sums = jnp.concatenate([total(SHARE + 16 * i, sources) for i in range(3)], axis=1)
        qkv[...] = sums
        out[...] = total(SHARE + 48, sources)
        gain_out[...] = gain_sums(sums, weights, gain, me)[0]
    for copy in copies:
        copy.wait()


def unpack(back, gain_t, qkv_t, gain_s, qkv_s):
    vmem = pl.BlockSpec(memory_space=pltpu.VMEM)
    return pl.pallas_call(
        unpack_kernel,
        in_specs=[vmem] * 5,
        out_specs=[pl.BlockSpec(memory_space=pl.ANY)] + [vmem] * 6,
        out_shape=(
            shaped(F32, 1, TOKENS, D),
            shaped(F32, 16, 3 * D),
            shaped(F32, 16, D),
            shaped(F32, 16, 3 * D),
            shaped(F32, 16, D),
            shaped(F32, 16),
            shaped(F32, 16),
        ),
        scratch_shapes=[pltpu.VMEM((4, 256, D), F32), pltpu.SemaphoreType.DMA((4,))],
        compiler_params=params(8),
    )(back, gain_t, qkv_t, gain_s, qkv_s)


def exchange(x):
    return lax.all_to_all(x, "frame", split_axis=0, concat_axis=0, tiled=True)


def per_device(latents, cotangent, gain_time, qkv_time, out_time, gain_space, qkv_space, out_space):
    gain_time, gain_space = gain_time.reshape(1, D), gain_space.reshape(1, D)
    moved = exchange(pack(latents, cotangent))
    *state, kept, given = run_main(
        moved, gain_time, qkv_time, out_time, gain_space, qkv_space, out_space
    )
    taken = lax.ppermute(given, "frame", [(i, i ^ 1) for i in range(FRAMES)])
    grads = run_input(*state, gain_time, qkv_time)
    back = exchange(join(grads, kept, taken))
    return tuple(unpack(back, gain_time, qkv_time, gain_space, qkv_space))


def solution(mesh):
    whole = P(("dp", "frame"), None, None)
    rows = P(("dp", "frame"), None)
    flat = P(("dp", "frame"))
    return jax.shard_map(
        per_device,
        mesh=mesh,
        in_specs=(whole, whole, P(), P(), P(), P(), P(), P()),
        out_specs=(whole, rows, rows, rows, rows, flat, flat),
        check_vma=False,
    )
```

```python
import jax
import jax.numpy as jnp
from jax import lax
from jax.experimental import pallas as pl
from jax.experimental.pallas import tpu as pltpu
from jax.sharding import PartitionSpec as P

HEADS = 8
HEAD_DIM = 32
D = 256
WIN = 8
HH = 32
WW = 32
FRAMES = 16
TOKENS = 1024
ROWS = 1024
SHARE = 64
GROUP = 128
HALF = 128
PACK = 4
CHUNK = 256
SPACE_STEP = 16
TIME_STEP = 8
EPSILON = 1e-06
SCALE = HEAD_DIM ** (-0.5)
LOG2E = 1.4426950408889634
F32 = jnp.float32
BF16 = jnp.bfloat16


def dot_nn(a, b):
    return lax.dot_general(a, b, (((1,), (0,)), ((), ())), preferred_element_type=F32)


def dot_nt(a, b):
    return lax.dot_general(a, b, (((1,), (1,)), ((), ())), preferred_element_type=F32)


def dot_tn(a, b):
    return lax.dot_general(a, b, (((0,), (0,)), ((), ())), preferred_element_type=F32)


def head_masks():
    lane = lax.broadcasted_iota(jnp.int32, (1, D), 1) // HEAD_DIM % PACK
    return [(lane == h).astype(F32).astype(BF16) for h in range(PACK)]


def spread(x, masks):
    return jnp.concatenate([x * m for m in masks], axis=0)


def halves(x):
    zero = jnp.zeros((x.shape[0], HALF), x.dtype)
    return jnp.concatenate(
        [
            jnp.concatenate([x[:, :HALF], zero], axis=1),
            jnp.concatenate([zero, x[:, HALF:]], axis=1),
        ],
        axis=0,
    )


def join_halves(x):
    n = x.shape[0] // 2
    return jnp.concatenate([x[:n, :HALF], x[n:, HALF:]], axis=1)


def each_token(f, x):
    n = x.shape[0] // 2
    return jnp.concatenate([f(x[:n]), f(x[n:])], axis=0)


def first_token():
    return lax.broadcasted_iota(jnp.int32, (32, 128), 1) < 64


def pair_scores(a, b):
    both = dot_nt(a, b)
    return jnp.where(first_token(), both[:32], both[32:])


def pair_mix(x, b):
    zero = jnp.zeros_like(x)
    one = first_token()
    both = jnp.concatenate([jnp.where(one, x, zero), jnp.where(one, zero, x)], axis=0)
    return each_token(join_halves, dot_nn(both.astype(BF16), b))


def flip_space(x):
    parts = []
    for pair in range(2):
        turned = x[:, HALF * pair : HALF * (pair + 1)].T
        parts += [turned[:SHARE], turned[SHARE:]]
    return jnp.concatenate(parts, axis=1)


def flip_time(x):
    turned = x.T
    blocks = [turned[16 * i : 16 * (i + 1)] for i in range(8)]
    lane = lax.broadcasted_iota(jnp.int32, (16, 128), 1) // 16
    for bit in range(3):
        step = 1 << bit
        upper = (lane // step) % 2 == 1
        for i in range(8):
            if not i & step:
                a, b = blocks[i], blocks[i + step]
                blocks[i] = jnp.where(upper, pltpu.roll(b, 16 * step, 1), a)
                blocks[i + step] = jnp.where(upper, b, pltpu.roll(a, 128 - 16 * step, 1))
    return jnp.concatenate(blocks, axis=0)


def softmax_keys(scores, axis):
    ex = jnp.exp2((scores - jnp.max(scores, axis=axis, keepdims=True)) * (SCALE * LOG2E))
    return ex * (1.0 / jnp.sum(ex, axis=axis, keepdims=True))


def score_grad(probs, dprobs, axis):
    weighted = probs * dprobs
    return weighted - probs * jnp.sum(weighted, axis=axis, keepdims=True)


def norm_factor(x):
    return lax.rsqrt(jnp.mean(x * x, -1, keepdims=True) + EPSILON)


def norm_back(dinput, normed, factor, gain):
    scaled = dinput * gain
    return factor * (scaled - normed * jnp.mean(scaled * normed, -1, keepdims=True))


def rows_of(c, size=CHUNK):
    return pl.ds(pl.multiple_of(c * size, size), size)


def swap_matrix():
    row = lax.broadcasted_iota(jnp.int32, (CHUNK, CHUNK), 0)
    col = lax.broadcasted_iota(jnp.int32, (CHUNK, CHUNK), 1)
    return (row == col % 16 * 16 + col // 16).astype(F32).astype(BF16)


def block(ref, c, base=0):
    rows = pl.ds(base + 16 * c, 16)
    return ref[:, rows, :].reshape(CHUNK, ref.shape[2])


def put_block(ref, c, x):
    ref[:, pl.ds(16 * c, 16), :] = x.reshape(FRAMES, 16, x.shape[1])


def main_kernel(
    moved, gain_t, qkv_t, out_t, gain_s, qkv_s, out_s, xs, dproj, dmid, kept, given,
    in_t, proj_t, probs_t, mixed_t, middle, in_s, proj_s, mixed_s, dmix_s, dmix_t, dproj_s, dmid_b, parts,
):
    masks = head_masks()

    def strided(ref, first, count, stride):
        return jnp.concatenate(
            [ref[half, pl.ds(first, count, stride=stride), :] for half in range(2)], axis=1
        )

    swap = swap_matrix()

    chunks = range(ROWS // CHUNK)
    x = [dot_nn(swap, block(moved, c)) for c in chunks]
    inp = [(y * norm_factor(y) * gain_t[...]).astype(BF16) for y in x]
    proj = [dot_nn(y, qkv_t[...]).astype(BF16) for y in inp]
    for c in chunks:
        xs[rows_of(c), :] = x[c].astype(BF16)
        in_t[rows_of(c), :] = inp[c]
        proj_t[rows_of(c), :] = proj[c]

    def time_pairs(c):
        return [
            pl.ds(pl.multiple_of(c * TIME_STEP * GROUP + 32 * i, 32), 32)
            for i in range(4 * TIME_STEP)
        ]

    def load(ref, offset, rows):
        return [ref[r, offset : offset + D] for r in rows]

    def spread_pairs(xs):
        return [each_token(lambda t: spread(t, masks), x) for x in xs]

    def halves_pairs(xs):
        return [each_token(halves, x) for x in xs]

    def by_four(xs):
        return [jnp.concatenate(xs[i : i + 4], axis=0) for i in range(0, len(xs), 4)]

    def in_pairs(xs):
        return [x[32 * i : 32 * (i + 1)] for x in xs for i in range(4)]

    def time_forward(c, _):
        rows = time_pairs(c)
        q, k, v = (load(proj_t, D * i, rows) for i in range(3))
        qb = spread_pairs(q)
        scores = by_four([pair_scores(x, y) for x, y in zip(halves_pairs(k), qb)])
        probs = [softmax_keys(x.reshape(8, 16, 128), 1).reshape(GROUP, 128) for x in scores]
        turned = in_pairs([flip_time(x) for x in probs])
        vb = spread_pairs(v)
        mixed = [pair_mix(x, y) for x, y in zip(turned, vb)]
        for n in range(TIME_STEP):
            probs_t[rows_of(c * TIME_STEP + n, GROUP), :] = probs[n].astype(BF16)
        for r, x in zip(rows, mixed):
            mixed_t[r, :] = x.astype(BF16)
        return _

    lax.fori_loop(0, ROWS // GROUP // TIME_STEP, time_forward, 0)

    dmix = [dot_nt(block(moved, c, SHARE), out_s[...]).astype(BF16) for c in chunks]
    mid = [xs[rows_of(c), :].astype(F32) + dot_nn(mixed_t[rows_of(c), :], out_t[...]) for c in chunks]
    mid = [dot_nn(swap, y.astype(BF16)) for y in mid]
    inp = [(y * norm_factor(y) * gain_s[...]).astype(BF16) for y in mid]
    proj = [dot_nn(y, qkv_s[...]).astype(BF16) for y in inp]
    for c in chunks:
        put_block(dmix_s, c, dmix[c])
        put_block(middle, c, mid[c])
        put_block(in_s, c, inp[c])
        put_block(proj_s, c, proj[c])

    def space(c, _):
        rows = [c * SPACE_STEP + i for i in range(SPACE_STEP)]
        q, k, v = ([proj_s[r, :, D * i : D * (i + 1)] for r in rows] for i in range(3))
        do = [dmix_s[r] for r in rows]

        def split(x):
            return x.reshape(2, SHARE, D)

        def turn(x):
            return jnp.concatenate([flip_space(x[:SHARE]), flip_space(x[SHARE:])], axis=0)

        qb = [spread(x, masks) for x in q]
        scores = [split(dot_nt(halves(x), y)) for x, y in zip(k, qb)]
        dob = [spread(x, masks) for x in do]
        dprobs = [split(dot_nt(halves(x), y)) for x, y in zip(v, dob)]
        probs = [softmax_keys(x, 1) for x in scores]
        probs_b = [x.astype(BF16).reshape(2 * SHARE, D) for x in probs]
        ds = [score_grad(x, y, 1).astype(BF16).reshape(2 * SHARE, D) for x, y in zip(probs, dprobs)]
        turned = [turn(x) for x in probs_b]
        ds_turned = [turn(x) for x in ds]
        dv = [join_halves(dot_nn(x, y)) for x, y in zip(probs_b, dob)]
        dk = [join_halves(dot_nn(x, y)) * SCALE for x, y in zip(ds, qb)]
        mixed = [join_halves(dot_nn(x, spread(y, masks))) for x, y in zip(turned, v)]
        dq = [join_halves(dot_nn(x, spread(y, masks))) * SCALE for x, y in zip(ds_turned, k)]
        for n, r in enumerate(rows):
            mixed_s[r] = mixed[n].astype(BF16)
            for i, grad in enumerate((dq, dk, dv)):
                dproj_s[r, :, D * i : D * (i + 1)] = grad[n].astype(BF16)
        return _

    lax.fori_loop(0, FRAMES // SPACE_STEP, space, 0)

    def place(kind, first, sums):
        sums = sums.astype(BF16)
        for i in range(sums.shape[1] // D):
            for d in range(FRAMES):
                parts[kind, d, first + 16 * i : first + 16 * (i + 1), :] = sums[
                    16 * d : 16 * (d + 1), D * i : D * (i + 1)
                ]

    def flat(ref):
        return ref[...].reshape(ROWS, ref.shape[2])

    place(1, 0, dot_tn(flat(in_s), flat(dproj_s)))
    place(1, 48, dot_tn(flat(mixed_s), moved[:, SHARE:, :].reshape(ROWS, D)))

    dinput = [dot_nt(block(dproj_s, c), qkv_s[...]) for c in chunks]
    mid = [block(middle, c) for c in chunks]
    factor = [norm_factor(y) for y in mid]
    normed = [y * f for y, f in zip(mid, factor)]
    dnorm = [norm_back(d, n, f, gain_s[...]) for d, n, f in zip(dinput, normed, factor)]
    dm = [block(moved, c, SHARE).astype(F32) + dnorm[c] for c in chunks]
    dm_b = [dot_nn(swap, y.astype(BF16)).astype(BF16) for y in dm]
    dmix = [dot_nt(y, out_t[...]).astype(BF16) for y in dm_b]
    for c in chunks:
        put_block(dmid, c, dm[c])
        dmid_b[rows_of(c), :] = dm_b[c]
        dmix_t[rows_of(c), :] = dmix[c]

    def time_back(c, _):
        rows = time_pairs(c)
        q, k, v = (load(proj_t, D * i, rows) for i in range(3))
        do = load(dmix_t, 0, rows)
        groups = [rows_of(c * TIME_STEP + n, GROUP) for n in range(TIME_STEP)]
        probs = [probs_t[g, :].astype(F32) for g in groups]
        dob = spread_pairs(do)
        dprobs = by_four([pair_scores(x, y) for x, y in zip(halves_pairs(v), dob)])
        ds = [
            score_grad(x.reshape(8, 16, 128), y.reshape(8, 16, 128), 1).reshape(GROUP, 128)
            for x, y in zip(probs, dprobs)
        ]
        turned = in_pairs([flip_time(x) for x in ds])
        dv = [pair_mix(x, y) for x, y in zip(in_pairs(probs), dob)]
        dk = [pair_mix(x, y) * SCALE for x, y in zip(in_pairs(ds), spread_pairs(q))]
        dq = [pair_mix(x, y) * SCALE for x, y in zip(turned, spread_pairs(k))]
        for n, r in enumerate(rows):
            for i, grad in enumerate((dq, dk, dv)):
                dproj[r, D * i : D * (i + 1)] = grad[n].astype(BF16)
        return _

    lax.fori_loop(0, ROWS // GROUP // TIME_STEP, time_back, 0)

    place(0, 0, dot_tn(in_t[...], dproj[...]))
    place(0, 48, dot_tn(mixed_t[...], dmid_b[...]))

    core = lax.axis_index("frame") % 2
    kept[...] = parts[core]
    given[...] = parts[1 - core]


def input_kernel(xs, dproj, dmid, gain_t, qkv_t, sent):
    swap = swap_matrix()
    chunks = range(ROWS // CHUNK)
    dinput = [dot_nt(dproj[rows_of(c), :], qkv_t[...]) for c in chunks]
    x = [xs[rows_of(c), :].astype(F32) for c in chunks]
    factor = [norm_factor(y) for y in x]
    normed = [y * f for y, f in zip(x, factor)]
    dnorm = [norm_back(d, n, f, gain_t[...]) for d, n, f in zip(dinput, normed, factor)]
    dnorm = [dot_nn(swap, y.astype(BF16)) for y in dnorm]
    for c in chunks:
        put_block(sent, c, (block(dmid, c) + dnorm[c]).astype(BF16))


def join_kernel(grads, kept, taken, sent):
    sent[:, :SHARE, :] = grads[...]
    sent[:, SHARE:, :] = (kept[...].astype(F32) + taken[...].astype(F32)).astype(BF16)


def shaped(kind, *shape):
    return jax.ShapeDtypeStruct(shape, kind)


def params(mebibytes):
    return pltpu.CompilerParams(vmem_limit_bytes=mebibytes * 1024 * 1024)


def run_main(moved, gain_t, qkv_t, out_t, gain_s, qkv_s, out_s):
    def rows(width, kind):
        return pltpu.VMEM((ROWS, width), kind)

    def frames(width, kind):
        return pltpu.VMEM((FRAMES, SHARE, width), kind)

    return pl.pallas_call(
        main_kernel,
        out_shape=(
            shaped(BF16, ROWS, D),
            shaped(BF16, ROWS, 3 * D),
            shaped(F32, FRAMES, SHARE, D),
            shaped(BF16, FRAMES, SHARE, D),
            shaped(BF16, FRAMES, SHARE, D),
        ),
        scratch_shapes=[
            rows(D, BF16),
            rows(3 * D, BF16),
            rows(128, BF16),
            rows(D, BF16),
            frames(D, F32),
            frames(D, BF16),
            frames(3 * D, BF16),
            frames(D, BF16),
            frames(D, BF16),
            rows(D, BF16),
            frames(3 * D, BF16),
            rows(D, BF16),
            pltpu.VMEM((2, FRAMES, SHARE, D), BF16),
        ],
        compiler_params=params(40),
        cost_estimate=pl.CostEstimate(
            flops=8 * 10**9, bytes_accessed=6 * 10**6, transcendentals=2 * 10**6
        ),
    )(moved, gain_t, qkv_t, out_t, gain_s, qkv_s, out_s)


def run_input(xs, dproj, dmid, gain_t, qkv_t):
    return pl.pallas_call(
        input_kernel,
        out_shape=shaped(BF16, FRAMES, SHARE, D),
        compiler_params=params(16),
        cost_estimate=pl.CostEstimate(flops=2 * 10**9, bytes_accessed=6 * 10**6, transcendentals=0),
    )(xs, dproj, dmid, gain_t, qkv_t)


def join(grads, kept, taken):
    return pl.pallas_call(
        join_kernel,
        out_shape=shaped(BF16, FRAMES, 2 * SHARE, D),
        compiler_params=params(8),
    )(grads, kept, taken)


def pack_kernel(latents, cotangent, packed, held, ready, sems, out_sems):
    copies = [
        [
            pltpu.make_async_copy(src.at[0, pl.ds(256 * wy, 256)], held.at[n, wy], sems.at[n, wy])
            for n, src in enumerate((latents, cotangent))
        ]
        for wy in range(4)
    ]
    for wy in range(4):
        for copy in copies[wy]:
            copy.start()
    outs = []
    for wy in range(4):
        for n in range(2):
            copies[wy][n].wait()
            for pair in range(4):
                rows = held[n, wy, 64 * pair : 64 * (pair + 1), :].astype(F32).reshape(2, 4, WIN, D)
                for wx in range(4):
                    both = jnp.concatenate([rows[0, wx], rows[1, wx]], axis=0).astype(BF16)
                    first = SHARE * n + 16 * pair
                    ready[4 * wy + wx, first : first + 16, :] = both
        outs.append(
            pltpu.make_async_copy(
                ready.at[pl.ds(4 * wy, 4)], packed.at[pl.ds(4 * wy, 4)], out_sems.at[wy]
            )
        )
        outs[wy].start()
    for copy in outs:
        copy.wait()


def pack(latents, cotangent):
    anywhere = pl.BlockSpec(memory_space=pl.ANY)
    return pl.pallas_call(
        pack_kernel,
        in_specs=[anywhere] * 2,
        out_specs=anywhere,
        out_shape=shaped(BF16, FRAMES, 2 * SHARE, D),
        scratch_shapes=[
            pltpu.VMEM((2, 4, 256, D), BF16),
            pltpu.VMEM((FRAMES, 2 * SHARE, D), BF16),
            pltpu.SemaphoreType.DMA((2, 4)),
            pltpu.SemaphoreType.DMA((4,)),
        ],
        compiler_params=params(60),
    )(latents, cotangent)


def gain_sums(sums, weights, gain, me):
    own = weights[pl.ds(pl.multiple_of(16 * me, 16), 16), :].astype(F32)
    column = jnp.sum(own * sums, axis=-1, keepdims=True)
    row = jnp.broadcast_to(column, (16, 128)).T[:1, :]
    turned = pltpu.roll(jnp.broadcast_to(gain[...], (8, D)), (D - 16 * me) % D, 1)
    return row / turned[:1, :16]


def unpack_kernel(
    back, gains_t, weights_t, gains_s, weights_s,
    grads, qkv_t, out_t, qkv_s, out_s, gain_t, gain_s, held, held_qkv, held_out, sems, weight_sems,
):
    copies = []
    for wy in range(4):
        for pair in range(4):
            rows = back[4 * wy : 4 * wy + 4, 16 * pair : 16 * (pair + 1), :].astype(F32)
            for wx in range(4):
                for i in range(2):
                    start = 64 * pair + 32 * i + WIN * wx
                    held[wy, start : start + WIN, :] = rows[wx, WIN * i : WIN * (i + 1)]
            if pair % 2:
                first = 64 * (pair - 1)
                copies.append(
                    pltpu.make_async_copy(
                        held.at[wy, pl.ds(first, 128)],
                        grads.at[0, pl.ds(256 * wy + first, 128)],
                        sems.at[wy, pair // 2],
                    )
                )
                copies[-1].start()
    inverse = (FRAMES * TOKENS) ** (-0.5)

    def total(first, sources):
        return sum(back[f, first : first + 16, :].astype(F32) for f in sources) * inverse

    me = lax.axis_index("frame")
    for core, qkv, out, gain, weights, gain_out in (
        (0, qkv_t, out_t, gains_t, weights_t, gain_t),
        (1, qkv_s, out_s, gains_s, weights_s, gain_s),
    ):
        sources = range(core, FRAMES, 2)
        sums = jnp.concatenate([total(SHARE + 16 * i, sources) for i in range(3)], axis=1)
        held_qkv[core] = sums
        held_out[core] = total(SHARE + 48, sources)
        for n, (src, dst) in enumerate(((held_qkv, qkv), (held_out, out))):
            copies.append(pltpu.make_async_copy(src.at[core], dst, weight_sems.at[core, n]))
            copies[-1].start()
        gain_out[...] = gain_sums(sums, weights, gain, me)[0]
    for copy in copies:
        copy.wait()


def unpack(back, gain_t, qkv_t, gain_s, qkv_s):
    vmem = pl.BlockSpec(memory_space=pltpu.VMEM)
    return pl.pallas_call(
        unpack_kernel,
        in_specs=[vmem] * 5,
        out_specs=[pl.BlockSpec(memory_space=pl.ANY)] * 5 + [vmem] * 2,
        out_shape=(
            shaped(F32, 1, TOKENS, D),
            shaped(F32, 16, 3 * D),
            shaped(F32, 16, D),
            shaped(F32, 16, 3 * D),
            shaped(F32, 16, D),
            shaped(F32, 16),
            shaped(F32, 16),
        ),
        scratch_shapes=[
            pltpu.VMEM((4, 256, D), F32),
            pltpu.VMEM((2, 16, 3 * D), F32),
            pltpu.VMEM((2, 16, D), F32),
            pltpu.SemaphoreType.DMA((4, 2)),
            pltpu.SemaphoreType.DMA((2, 2)),
        ],
        compiler_params=params(8),
    )(back, gain_t, qkv_t, gain_s, qkv_s)


def exchange(x):
    return lax.all_to_all(x, "frame", split_axis=0, concat_axis=0, tiled=True)


def per_device(latents, cotangent, gain_time, qkv_time, out_time, gain_space, qkv_space, out_space):
    gain_time, gain_space = gain_time.reshape(1, D), gain_space.reshape(1, D)
    moved = exchange(pack(latents, cotangent))
    *state, kept, given = run_main(
        moved, gain_time, qkv_time, out_time, gain_space, qkv_space, out_space
    )
    taken = lax.ppermute(given, "frame", [(i, i ^ 1) for i in range(FRAMES)])
    grads = run_input(*state, gain_time, qkv_time)
    back = exchange(join(grads, kept, taken))
    return tuple(unpack(back, gain_time, qkv_time, gain_space, qkv_space))


def solution(mesh):
    whole = P(("dp", "frame"), None, None)
    rows = P(("dp", "frame"), None)
    flat = P(("dp", "frame"))
    return jax.shard_map(
        per_device,
        mesh=mesh,
        in_specs=(whole, whole, P(), P(), P(), P(), P(), P()),
        out_specs=(whole, rows, rows, rows, rows, flat, flat),
        check_vma=False,
    )
```
